256 devices in a mesh: ctx: 16 (over y, x_hi, core), tp: 16 (over z, x_lo).
Axes of the slice: x: 4 (x_hi: 2, x_lo: 2; x = x_hi * 2 + x_lo), y: 4, z: 8, core: 2. Of those that a mesh axis runs over, the one named last changes fastest.
Arguments:
- query: bfloat16 [8192, 4096], P('ctx', 'tp'), may hold values from -200 to 200
- key: bfloat16 [8192, 1024], P('ctx'), may hold values from -8 to 8
- value: bfloat16 [8192, 1024], P('ctx'), may hold values from -6 to 6
- out_weight: bfloat16 [4096, 4096], P('tp'), may hold values from -0.75 to 0.75
- residual: bfloat16 [8192, 4096], P('ctx'), may hold values from -3 to 3
- norm_gain: float32 [4096], replicated, may hold values from 0.1 to 1.9
- w_zx: bfloat16 [4096, 2, 8192], P('ctx', None, 'tp'), may hold values from -0.09375 to 0.09375
- w_bc: bfloat16 [4096, 2, 1024], P('ctx'), may hold values from -0.09375 to 0.09375
- w_dt: bfloat16 [4096, 128], P('ctx', 'tp'), may hold values from -0.09375 to 0.09375
- conv_x_weight: float32 [4, 8192], P(None, 'tp'), may hold values from -3 to 3
- conv_x_bias: float32 [8192], P('tp'), may hold values from -3 to 3
- conv_bc_weight: float32 [4, 2, 1024], replicated, may hold values from -3 to 3
- conv_bc_bias: float32 [2, 1024], replicated, may hold values from -3 to 3
- dt_bias: float32 [128], P('tp'), may hold values from -4.5 to -3.5
- a_log: float32 [128], P('tp'), may hold values from -20 to 1
- d_skip: float32 [128], P('tp'), may hold values from 0.5 to 1.5
Outputs:
- stream: bfloat16 [8192, 4096], P('ctx', 'tp')
- gated: bfloat16 [8192, 8192], P('ctx', 'tp')
The draws below stay inside these ranges and needn't reach their ends.
All inputs are finite; a program needn't handle non-finite values.
Results may differ from the reference program's by a relative error of at most 0.029.
Values may be sent and summed in bfloat16 or wider, within the bound.
No kernel may reach another device: no remote copies, remote signals or barrier semaphores. Data moves between devices by JAX's collectives and lax.ppermute only.
A program may use at most 128 MiB of HBM per device.

```python
import math
import jax
import jax.numpy as jnp
from jax import lax

D = 4096
ATT_HEADS = 32
KV_HEADS = 8
HEAD_DIM = 128
SSM_HEADS = 128
SSM_HEAD_DIM = 64
STATE = 128
GROUPS = 8
CONV = 4
BLOCK = 128
TOKENS = 8192
INNER = 8192


def shared_keys(key):
    base = jnp.clip(jax.random.normal(jax.random.fold_in(key, 101), (TOKENS, KV_HEADS * HEAD_DIM), jnp.float32), -6.0, 6.0)
    positions = jnp.arange(TOKENS)
    twins = (positions % 211 == 5)[:, None]
    mixed = base
    return jnp.clip(jnp.where(twins, mixed, base), -8.0, 8.0)


def draw_key(key, part):
    keys_drawn = shared_keys(key)
    return keys_drawn.astype(jnp.bfloat16)


def draw_query(key, part):
    key = jax.random.fold_in(key, 7)
    drawn = jnp.clip(jax.random.normal(key, (TOKENS, ATT_HEADS * HEAD_DIM), jnp.float32), -6.0, 6.0)
    return drawn.astype(jnp.bfloat16)


def draw_a_log(key, part):
    key = jax.random.fold_in(key, 3)
    pick_key, spread_key, level_key = jax.random.split(key, 3)
    fast_share = 0.5
    chance = jax.random.uniform(pick_key, (SSM_HEADS,), jnp.float32)
    fast_rates = jnp.log(0.8) + jax.random.uniform(spread_key, (SSM_HEADS,), jnp.float32, -0.3, 0.3)
    levels = 0.3 + 1.2 * jax.random.uniform(level_key, (SSM_HEADS,), jnp.float32)
    slow_rates = jnp.log(levels / (0.03 * TOKENS))
    return jnp.where(chance < fast_share, fast_rates, slow_rates).astype(jnp.float32)


def block_levels(stream_key, extent, pieces, least, high):
    level = 1.0
    for dim, blocks in pieces:
        steps = jax.random.uniform(jax.random.fold_in(jax.random.fold_in(stream_key, 6), dim), (blocks,), jnp.float32, least / len(pieces), high / len(pieces))
        level = level * jnp.repeat(jnp.exp(steps), extent[dim] // blocks).reshape((-1,) + (1,) * (len(extent) - 1 - dim))
    return level


def gaussian(own_key, extent, spread, most, shards=(), held_as=jnp.bfloat16):
    entries = jax.random.normal(own_key, extent, jnp.float32) * spread
    if len(shards) > 0:
        entries = block_levels(own_key, extent, shards, -0.22, 0.18) * entries
    return jnp.clip(entries, min=-most, max=most).astype(held_as)


def setup_inputs(seed: int = 0) -> dict:
    keys = jax.random.split(jax.random.key(seed), 17)
    return {
        "query": draw_query(jax.random.fold_in(keys[16], 71), 0),
        "key": draw_key(jax.random.fold_in(keys[16], 71), 0),
        "value": gaussian(keys[2], (TOKENS, KV_HEADS * HEAD_DIM), 1.0, 6.0, ((0, 16),)),
        "out_weight": gaussian(keys[3], (ATT_HEADS * HEAD_DIM, D), (ATT_HEADS * HEAD_DIM // 64) ** -0.5, 0.75, ((0, 16),)),
        "residual": gaussian(keys[4], (TOKENS, D), 0.5, 3.0, ((0, 16),)),
        "norm_gain": jnp.clip(1.0 + 0.18 * jax.random.normal(keys[5], (D,), jnp.float32), 0.1, 1.9),
        "w_zx": gaussian(keys[6], (D, 2, INNER), D ** -0.5, 0.09375, ((0, 16), (2, 16))),
        "w_bc": gaussian(keys[7], (D, 2, GROUPS * STATE), D ** -0.5, 0.09375, ((0, 16),)),
        "w_dt": gaussian(keys[8], (D, SSM_HEADS), D ** -0.5, 0.09375, ((0, 16), (1, 16))),
        "conv_x_weight": gaussian(keys[9], (CONV, INNER), CONV ** -0.5, 3.0, ((1, 16),), jnp.float32),
        "conv_x_bias": gaussian(keys[10], (INNER,), 0.5, 3.0, ((0, 16),), jnp.float32),
        "conv_bc_weight": gaussian(keys[11], (CONV, 2, GROUPS * STATE), CONV ** -0.5, 3.0, (), jnp.float32),
        "conv_bc_bias": gaussian(keys[12], (2, GROUPS * STATE), 0.5, 3.0, (), jnp.float32),
        "dt_bias": jnp.clip(-4.5 + 1.0 * jax.random.uniform(keys[13], (SSM_HEADS,), jnp.float32) ** block_levels(keys[13], (SSM_HEADS,), ((0, 16),), -0.2, 0.2), -4.5, -3.5),
        "a_log": draw_a_log(jax.random.fold_in(keys[16], 71), 0),
        "d_skip": jnp.clip(0.5 + 1.0 * jax.random.uniform(keys[15], (SSM_HEADS,), jnp.float32) ** block_levels(keys[15], (SSM_HEADS,), ((0, 16),), -0.2, 0.2), 0.5, 1.5),
    }


NEG_BIG = -1e+30
EPSILON = 1e-05
HIGHEST_PRECISION = lax.Precision.HIGHEST

def silu_f32(values):
    return values / (1.0 + jnp.exp(-values))

def attend_rows(query, key, value):
    per_kv = ATT_HEADS // KV_HEADS
    queries = query.reshape(TOKENS, KV_HEADS, per_kv, HEAD_DIM)
    keys_all = key.reshape(TOKENS, KV_HEADS, HEAD_DIM).astype(jnp.float32)
    values_all = value.reshape(TOKENS, KV_HEADS, HEAD_DIM).astype(jnp.float32)
    row_block = 256 if TOKENS % 256 == 0 else TOKENS
    scaling = 1.0 / math.sqrt(HEAD_DIM)
    key_pos = jnp.arange(TOKENS, dtype=jnp.int32)

    def one_block(block_index):
        first = (block_index * row_block).astype(jnp.int32)
        query_block = lax.dynamic_slice_in_dim(queries, first, row_block, 0).astype(jnp.float32)
        scores = jnp.einsum('qkgd,nkd->kgqn', query_block, keys_all) * scaling
        query_pos = first + jnp.arange(row_block, dtype=jnp.int32)
        visible = key_pos[None, :] <= query_pos[:, None]
        masked = jnp.where(visible, scores, NEG_BIG)
        row_max = lax.optimization_barrier(jnp.max(masked, axis=-1, keepdims=True))
        weights = jnp.where(visible, jnp.exp(masked - row_max), 0.0)
        weight_sum = lax.optimization_barrier(jnp.sum(weights, axis=-1))
        probs = lax.optimization_barrier(weights.astype(jnp.bfloat16)).astype(jnp.float32)
        mixed = jnp.einsum('kgqn,nkd->kgqd', probs, values_all)
        context = (mixed / weight_sum[..., None]).astype(jnp.bfloat16)
        return jnp.transpose(context, (2, 0, 1, 3)).reshape(row_block, ATT_HEADS * HEAD_DIM)
    blocks = lax.map(one_block, jnp.arange(TOKENS // row_block, dtype=jnp.int32))
    return blocks.reshape(TOKENS, ATT_HEADS * HEAD_DIM)

def causal_conv(padded, weight, bias, row_count):
    summed = bias[None, :] + weight[0][None, :] * padded[0:row_count].astype(jnp.float32)
    for offset in range(1, CONV):
        summed = summed + weight[offset][None, :] * padded[offset:offset + row_count].astype(jnp.float32)
    return silu_f32(summed).astype(jnp.bfloat16)

def ssd_block(carried_state, inputs):
    x_block, b_block, c_block, dt_block, rate_block = inputs
    length = x_block.shape[0]
    per_group = x_block.shape[1] // b_block.shape[1]
    b_float = b_block.astype(jnp.float32)
    c_float = c_block.astype(jnp.float32)
    b_heads = jnp.repeat(b_float, per_group, axis=1)
    c_heads = jnp.repeat(c_float, per_group, axis=1)
    cumulative = jnp.cumsum(rate_block, axis=0)
    lower_part = (jnp.arange(length)[:, None] >= jnp.arange(length)[None, :])[:, :, None]
    log_gaps = cumulative[:, None, :] - cumulative[None, :, :]
    decays = jnp.where(lower_part, jnp.exp(jnp.where(lower_part, log_gaps, 0.0)), 0.0)
    intersections = jnp.einsum('ign,jgn->ijg', c_float, b_float, precision=HIGHEST_PRECISION)
    intersections = jnp.repeat(intersections, per_group, axis=2)
    scaled_x = x_block.astype(jnp.float32) * dt_block[:, :, None]
    outputs = jnp.einsum('ijh,jhp->ihp', decays * intersections, scaled_x, precision=HIGHEST_PRECISION)
    readout = jnp.einsum('ihn,hnp->ihp', c_heads, carried_state, precision=HIGHEST_PRECISION)
    outputs = outputs + jnp.exp(cumulative)[:, :, None] * readout
    remaining = jnp.exp(cumulative[-1][None, :] - cumulative)
    added = jnp.einsum('jhn,jhp->hnp', b_heads * remaining[:, :, None], scaled_x, precision=HIGHEST_PRECISION)
    new_state = jnp.exp(cumulative[-1])[:, None, None] * carried_state + added
    return (new_state, outputs)

def ssd_scan(x_heads, b_in, c_in, dt_values, rate, start_state):
    block_count = x_heads.shape[0] // BLOCK

    def by_blocks(array):
        return array.reshape((block_count, BLOCK) + array.shape[1:])
    final_state, outputs = lax.scan(ssd_block, start_state, (by_blocks(x_heads), by_blocks(b_in), by_blocks(c_in), by_blocks(dt_values), by_blocks(rate)))
    return (outputs.reshape(x_heads.shape), final_state)

def reference(query, key, value, out_weight, residual, norm_gain, w_zx, w_bc, w_dt, conv_x_weight, conv_x_bias, conv_bc_weight, conv_bc_bias, dt_bias, a_log, d_skip):
    context = attend_rows(query, key, value)
    attended = jnp.dot(context, out_weight, preferred_element_type=jnp.float32)
    stream = (residual.astype(jnp.float32) + attended).astype(jnp.bfloat16)
    stream_f32 = stream.astype(jnp.float32)
    inverse = lax.rsqrt(lax.optimization_barrier(jnp.mean(stream_f32 * stream_f32, axis=-1, keepdims=True)) + EPSILON)
    normed = (stream_f32 * inverse * norm_gain[None, :]).astype(jnp.bfloat16)
    zx_proj = jnp.dot(normed, w_zx.reshape(D, 2 * INNER), preferred_element_type=jnp.float32).astype(jnp.bfloat16)
    bc_pre = jnp.dot(normed, w_bc.reshape(D, 2 * GROUPS * STATE), preferred_element_type=jnp.float32).astype(jnp.bfloat16)
    dt_raw = jnp.dot(normed, w_dt, preferred_element_type=jnp.float32).astype(jnp.bfloat16)
    gate_in = zx_proj[:, :INNER]
    x_pre = zx_proj[:, INNER:]
    x_padded = jnp.concatenate([jnp.zeros((CONV - 1, INNER), jnp.bfloat16), x_pre], axis=0)
    x_conv = causal_conv(x_padded, conv_x_weight, conv_x_bias, TOKENS)
    bc_padded = jnp.concatenate([jnp.zeros((CONV - 1, 2 * GROUPS * STATE), jnp.bfloat16), bc_pre], axis=0)
    bc_conv = causal_conv(bc_padded, conv_bc_weight.reshape(CONV, 2 * GROUPS * STATE), conv_bc_bias.reshape(2 * GROUPS * STATE), TOKENS)
    b_in = bc_conv[:, :GROUPS * STATE].reshape(TOKENS, GROUPS, STATE)
    c_in = bc_conv[:, GROUPS * STATE:].reshape(TOKENS, GROUPS, STATE)
    dt_values = jax.nn.softplus(dt_raw.astype(jnp.float32) + dt_bias[None, :])
    rate = -jnp.exp(a_log)[None, :] * dt_values
    x_heads = x_conv.reshape(TOKENS, SSM_HEADS, SSM_HEAD_DIM)
    start_state = jnp.zeros((SSM_HEADS, STATE, SSM_HEAD_DIM), jnp.float32)
    y_heads, final_state = ssd_scan(x_heads, b_in, c_in, dt_values, rate, start_state)
    y_heads = y_heads + d_skip[None, :, None] * x_heads.astype(jnp.float32)
    gated = (y_heads.reshape(TOKENS, INNER) * silu_f32(gate_in.astype(jnp.float32))).astype(jnp.bfloat16)
    return (stream, gated)
```

```python
import functools
import math

import jax
import jax.numpy as jnp
from jax import lax
from jax.experimental import pallas as pl
from jax.experimental.pallas import tpu as pltpu
from jax.sharding import PartitionSpec as P

D = 4096
HEAD_DIM = 128
SSM_HEAD_DIM = 64
STATE = 128
CONV = 4
BLOCK = 128
NEG_BIG = -1e30
EPSILON = 1e-05
HIGHEST = lax.Precision.HIGHEST
F32 = jnp.float32
BF16 = jnp.bfloat16
MIB = 1024 * 1024

Y, Z = 4, 8
ROWS = 512
HALF = 256
TAIL = 16
MSG = STATE + 16


def ctx_permute(block, move):
    return lax.ppermute(block, "ctx", [(i, move(i)) for i in range(16)])


def tp_permute(block, move):
    return lax.ppermute(block, "tp", [(i, move(i)) for i in range(16)])


def y_step(block, d):
    return ctx_permute(block, lambda i: (i + 4 * d) % 16)


def z_step(block, d):
    return tp_permute(block, lambda i: (i + 2 * d) % 16)


def x_swap(block):
    return tp_permute(block, lambda i: i ^ 1)


def dot(a, b, dims=((1,), (0,)), precision=None):
    return lax.dot_general(a, b, (dims, ((), ())), precision=precision, preferred_element_type=F32)


def whole(memory=pltpu.VMEM):
    return pl.BlockSpec(memory_space=memory)


def attend_kernel(place, q_own, q_other, *refs):
    pieces, (out, kv, sems, top, total, acc) = refs[:10], refs[10:]
    me = place[0]
    first_row = place[1]
    homes = ((0, 2), (6, 2), (2, 2), (4, 1), (5, 1), (8, 2), (14, 2), (10, 2), (12, 1), (13, 1))
    copies = [
        pltpu.make_async_copy(piece, kv.at[pl.ds(at, n)], sems.at[i])
        for i, (piece, (at, n)) in enumerate(zip(pieces, homes))
    ]
    for copy in copies:
        copy.start()
    for copy in copies:
        copy.wait()
    unit = math.log2(math.e) / math.sqrt(HEAD_DIM)
    top[...] = jnp.full(top.shape, NEG_BIG, F32)
    total[...] = jnp.zeros(total.shape, F32)
    acc[...] = jnp.zeros(acc.shape, F32)

    def block(slot, masked):
        keys = kv[slot, 0:ROWS, :]
        values = jnp.concatenate(
            [kv[slot, ROWS + HEAD_DIM * j : ROWS + HEAD_DIM * (j + 1), :] for j in range(4)], axis=1
        )
        for h in range(4):
            source = q_own if h < 2 else q_other
            queries = source[:, (h % 2) * HEAD_DIM : (h % 2 + 1) * HEAD_DIM]
            scores = dot(keys, queries, ((1,), (1,)))
            if masked:
                key_at = lax.broadcasted_iota(jnp.int32, scores.shape, 0)
                row_at = lax.broadcasted_iota(jnp.int32, scores.shape, 1) + first_row
                scores = jnp.where(key_at <= row_at, scores, NEG_BIG)
            old = top[h]
            new = jnp.maximum(old, jnp.max(scores, axis=0, keepdims=True))
            weights = jnp.exp2((scores - new) * unit)
            factor = jnp.exp2((old - new) * unit)
            total[h] = total[h] * factor + jnp.sum(weights, axis=0, keepdims=True)
            acc[h] = acc[h] * factor + dot(values, weights.astype(BF16))
            top[h] = new

    block(0, True)

    @pl.loop(0, me)
    def _(i):
        apart = jnp.bitwise_and(i // 4 - me // 4, 3)
        crossed = jnp.bitwise_xor(jnp.bitwise_and(i, 3), jnp.bitwise_and(me, 3))
        slot = jnp.bitwise_and(crossed, 1) * 8 + apart * 2 + crossed // 2
        block(slot, False)

    for h in range(4):
        out[:, h * HEAD_DIM : (h + 1) * HEAD_DIM] = (acc[h] / total[h]).T.astype(BF16)


def attend(place, q_own, q_other, pieces):
    return pl.pallas_call(
        attend_kernel,
        out_shape=jax.ShapeDtypeStruct((HALF, 4 * HEAD_DIM), BF16),
        in_specs=[whole(pltpu.SMEM), whole(), whole()] + [whole(pl.ANY)] * 10,
        out_specs=whole(),
        scratch_shapes=[
            pltpu.VMEM((16, 2 * ROWS, HEAD_DIM), BF16),
            pltpu.SemaphoreType.DMA((10,)),
            pltpu.VMEM((4, 1, HALF), F32),
            pltpu.VMEM((4, 1, HALF), F32),
            pltpu.VMEM((4, HEAD_DIM, HALF), F32),
        ],
        compiler_params=pltpu.CompilerParams(vmem_limit_bytes=32 * MIB),
        cost_estimate=pl.CostEstimate(
            flops=4_300_000_000, bytes_accessed=5_000_000, transcendentals=8_400_000
        ),
        name="attend",
    )(place, q_own, q_other, *pieces)


def gather_keys(message):
    across = ctx_permute(message, lambda i: i ^ 2)
    mine = jnp.stack([message, across])
    below, above = y_step(mine, 1), y_step(mine, -1)
    far_0 = y_step(below[0:1], 1)
    far_1 = y_step(above[1:2], -1)
    held = [mine, below, above, far_0, far_1]
    return held + [ctx_permute(part, lambda i: i ^ 1) for part in held]


def sum_over_z(context, weight):
    wide = weight.shape[1] // Z
    half = wide // 2

    def part(k):
        return dot(context, weight[:, k * wide : (k + 1) * wide])

    up = z_step(part(4)[:, :half].astype(BF16), 1)
    down = z_step(part(4)[:, half:].astype(BF16), -1)
    third, fifth = part(3), part(5)
    up = jnp.concatenate([third[:, :half] + up.astype(F32), third[:, half:]], axis=1)
    down = jnp.concatenate([fifth[:, :half], fifth[:, half:] + down.astype(F32)], axis=1)
    for k in (2, 1, 0):
        up, down = z_step(up.astype(BF16), 1), z_step(down.astype(BF16), -1)
        if k:
            up, down = part(k) + up.astype(F32), part(8 - k) + down.astype(F32)
    return part(0) + up.astype(F32) + down.astype(F32)


def gather_rows(piece):
    half = piece.shape[1] // 2
    near = {0: piece}
    up = down = piece
    for k in (1, 2, 3):
        up, down = z_step(up, 1), z_step(down, -1)
        near[8 - k], near[k] = up, down
    far = jnp.concatenate([z_step(up[:, :half], 1), z_step(down[:, half:], -1)], axis=1)
    near[4] = far
    other = {0: x_swap(piece)}
    for k in (1, 7):
        other[k] = z_step(other[0], 1 if k == 7 else -1)
    for k in (2, 6, 3, 5, 4):
        other[k] = x_swap(near[k])
    return [near[k] for k in range(Z)], [other[k] for k in range(Z)]


def norm_kernel(place, gain, *refs):
    near, other, out = refs[:Z], refs[Z : 2 * Z], refs[2 * Z]
    z, x_lo = place[2], place[3]
    wide = D // Z
    for blocks, start in ((near, x_lo * HALF), (other, (1 - x_lo) * HALF)):
        square = jnp.zeros((HALF, wide), F32)
        for k in range(Z):
            value = blocks[k][...].astype(F32)
            square = square + value * value
        mean = jnp.sum(square, axis=1, keepdims=True) * (1.0 / D)
        inverse = lax.rsqrt(mean + EPSILON)
        for k in range(Z):
            at = pl.multiple_of(jnp.bitwise_and(z + k, Z - 1) * wide, wide)
            value = blocks[k][...].astype(F32) * inverse * gain[:, pl.ds(at, wide)]
            out[pl.ds(pl.multiple_of(start, HALF), HALF), pl.ds(at, wide)] = value.astype(BF16)


def norm(place, gain, near, other):
    return pl.pallas_call(
        norm_kernel,
        out_shape=jax.ShapeDtypeStruct((ROWS, D), BF16),
        in_specs=[whole(pltpu.SMEM)] + [whole()] * (1 + 2 * Z),
        out_specs=whole(),
        compiler_params=pltpu.CompilerParams(vmem_limit_bytes=32 * MIB),
        cost_estimate=pl.CostEstimate(
            flops=10_000_000, bytes_accessed=8_400_000, transcendentals=ROWS
        ),
        name="norm",
    )(place, gain, *near, *other)


INNER = 512
WIDE = INNER + 2 * STATE


def silu(values):
    return values / (1.0 + jnp.exp(-values))


def per_channel(values):
    head = lax.broadcasted_iota(jnp.int32, (128, INNER), 0)
    channel = lax.broadcasted_iota(jnp.int32, (128, INNER), 1)
    spread = (head == channel // SSM_HEAD_DIM).astype(BF16)
    return dot(values.astype(BF16), spread)


def conv_kernel(proj, tail, weight, bias, dt_bias, a_log, x_out, bc_out, cum_out, dt_out, msg, pad):
    pad[0:TAIL, :] = tail[...].astype(F32)
    pad[TAIL:, :] = proj[:, 0:WIDE].astype(F32)
    summed = bias[...] + weight[0:1, :] * pad[pl.ds(TAIL - CONV + 1, ROWS), :]
    for k in range(1, CONV):
        summed = summed + weight[k : k + 1, :] * pad[pl.ds(TAIL - CONV + 1 + k, ROWS), :]
    conv = silu(summed).astype(BF16)
    x_out[...] = conv[:, :INNER]
    bc_out[...] = conv[:, INNER:]
    raw = proj[:, WIDE:].astype(F32) + dt_bias[...]
    step = jnp.maximum(raw, 0.0) + jnp.log1p(jnp.exp(-jnp.abs(raw)))
    dt_out[...] = step
    rate = -jnp.exp(a_log[...]) * step
    later = lax.broadcasted_iota(jnp.int32, (BLOCK, BLOCK), 0)
    earlier = lax.broadcasted_iota(jnp.int32, (BLOCK, BLOCK), 1)
    lower = (later >= earlier).astype(F32)
    base = jnp.zeros((1, 128), F32)
    for k in range(ROWS // BLOCK):
        rows = slice(k * BLOCK, (k + 1) * BLOCK)
        here = dot(lower, rate[rows], precision=HIGHEST) + base
        cum_out[rows, :] = here
        base = here[BLOCK - 1 : BLOCK, :]
    left = step * jnp.exp(base - cum_out[...])
    weighted = (x_out[...].astype(F32) * per_channel(left)).astype(BF16)
    msg[0:STATE, :] = dot(bc_out[:, :STATE], weighted, ((0,), (0,))).astype(BF16)
    msg[STATE:, :] = per_channel(jnp.broadcast_to(jnp.exp(base), (16, 128))).astype(BF16)


def conv_and_state(proj, tail, weight, bias, dt_bias, a_log):
    return pl.pallas_call(
        conv_kernel,
        out_shape=(
            jax.ShapeDtypeStruct((ROWS, INNER), BF16),
            jax.ShapeDtypeStruct((ROWS, 2 * STATE), BF16),
            jax.ShapeDtypeStruct((ROWS, 128), F32),
            jax.ShapeDtypeStruct((ROWS, 128), F32),
            jax.ShapeDtypeStruct((MSG, INNER), BF16),
        ),
        in_specs=[whole()] * 6,
        out_specs=(whole(),) * 5,
        scratch_shapes=[pltpu.VMEM((ROWS + TAIL, WIDE), F32)],
        compiler_params=pltpu.CompilerParams(vmem_limit_bytes=32 * MIB),
        cost_estimate=pl.CostEstimate(
            flops=200_000_000, bytes_accessed=3_000_000, transcendentals=800_000
        ),
        name="conv_and_state",
    )(proj, tail, weight, bias, dt_bias, a_log)


def scan_kernel(x_ref, bc, cum, step, d_skip, out):
    lower = lax.broadcasted_iota(jnp.int32, (BLOCK, BLOCK), 0) >= lax.broadcasted_iota(
        jnp.int32, (BLOCK, BLOCK), 1
    )
    low_lane = lax.broadcasted_iota(jnp.int32, (BLOCK, 128), 1) < SSM_HEAD_DIM
    state = None
    for k in range(ROWS // BLOCK):
        rows = slice(k * BLOCK, (k + 1) * BLOCK)
        b, c = bc[rows, :STATE], bc[rows, STATE:]
        x = x_ref[rows, :]
        here = cum[rows, :]
        here_t, step_t = here.T, step[rows, :].T
        met = jnp.where(lower, dot(c, b, ((1,), (1,))), 0.0)
        parts = []
        for pair in range(4):
            left = []
            for h in (2 * pair, 2 * pair + 1):
                gap = jnp.minimum(here[:, h : h + 1] - here_t[h : h + 1, :], 0.0)
                left.append((met * jnp.exp(gap) * step_t[h : h + 1, :]).astype(BF16))
            xs = x[:, pair * 128 : (pair + 1) * 128]
            none = jnp.zeros_like(xs)
            right = jnp.concatenate([jnp.where(low_lane, xs, none), jnp.where(low_lane, none, xs)], 0)
            parts.append(dot(jnp.concatenate(left, axis=1), right))
        y = jnp.concatenate(parts, axis=1)
        last = here[BLOCK - 1 : BLOCK, :]
        if k:
            start = cum[k * BLOCK - 1 : k * BLOCK, :]
            y = y + dot(c, state.astype(BF16)) * per_channel(jnp.exp(here - start))
        out[rows, :] = y + d_skip[...] * x.astype(F32)
        if k < ROWS // BLOCK - 1:
            weighted = per_channel(step[rows, :] * jnp.exp(last - here)) * x.astype(F32)
            added = dot(b, weighted.astype(BF16), ((0,), (0,)))
            if k:
                kept = per_channel(jnp.broadcast_to(jnp.exp(last - start), (8, 128)))[0:1, :]
                state = state * kept + added
            else:
                state = added


def local_scan(x, bc, cum, step, d_skip):
    return pl.pallas_call(
        scan_kernel,
        out_shape=jax.ShapeDtypeStruct((ROWS, INNER), F32),
        in_specs=[whole()] * 5,
        out_specs=whole(),
        compiler_params=pltpu.CompilerParams(vmem_limit_bytes=32 * MIB),
        cost_estimate=pl.CostEstimate(
            flops=400_000_000, bytes_accessed=3_000_000, transcendentals=600_000
        ),
        name="local_scan",
    )(x, bc, cum, step, d_skip)


def gate_kernel(y, bc, cum, state, gate, out):
    carried = dot(bc[:, STATE:], state[...]) * per_channel(jnp.exp(cum[...]))
    out[...] = ((y[...] + carried) * silu(gate[...].astype(F32))).astype(BF16)


def finish(y, bc, cum, state, gate):
    return pl.pallas_call(
        gate_kernel,
        out_shape=jax.ShapeDtypeStruct((ROWS, INNER), BF16),
        in_specs=[whole()] * 5,
        out_specs=whole(),
        compiler_params=pltpu.CompilerParams(vmem_limit_bytes=32 * MIB),
        cost_estimate=pl.CostEstimate(
            flops=70_000_000, bytes_accessed=3_500_000, transcendentals=600_000
        ),
        name="gate",
    )(y, bc, cum, state, gate)


def then(earlier, later):
    return (earlier[0] * later[1] + later[0], earlier[1] * later[1])


def unpack(message):
    values = message.astype(F32)
    return values[:STATE], values[STATE : STATE + 1]


def earlier_state(message, ctx):
    position = jnp.bitwise_and(ctx, 3)
    met = [message] + [ctx_permute(message, lambda i, d=d: i ^ d) for d in (1, 2, 3)]
    met = [unpack(part) for part in met]
    none = (jnp.zeros((STATE, INNER), F32), jnp.ones((1, INNER), F32))
    before, block = none, none
    for p in range(4):
        apart = jnp.bitwise_xor(position, p)
        part = tuple(
            jnp.where(apart == 0, a, jnp.where(apart == 1, b, jnp.where(apart == 2, c, d)))
            for a, b, c, d in zip(*met)
        )
        follow = then(before, part)
        before = tuple(jnp.where(p < position, a, b) for a, b in zip(follow, before))
        block = then(block, part)
    packed = jnp.concatenate([block[0], jnp.broadcast_to(block[1], (16, INNER))]).astype(BF16)
    blocks = []
    for d in (1, 2, 3):
        pairs = [(i, i + 4 * d) for i in range(16) if i + 4 * d < 16]
        blocks.append(unpack(lax.ppermute(packed, "ctx", pairs)))
    near, mid, far = blocks
    incoming = then(then(far, mid), near)[0]
    return (incoming * before[1] + before[0]).astype(BF16)


def shards(
    query,
    key,
    value,
    out_weight,
    residual,
    norm_gain,
    w_zx,
    w_bc,
    w_dt,
    conv_x_weight,
    conv_x_bias,
    conv_bc_weight,
    conv_bc_bias,
    dt_bias,
    a_log,
    d_skip,
):
    tp, ctx = lax.axis_index("tp"), lax.axis_index("ctx")
    z, x_lo = tp // 2, jnp.bitwise_and(tp, 1)
    place = jnp.stack([ctx, x_lo * HALF, z, x_lo]).astype(jnp.int32)

    keys = lax.dynamic_slice_in_dim(key, z * HEAD_DIM, HEAD_DIM, 1)
    values = lax.dynamic_slice_in_dim(value, z * HEAD_DIM, HEAD_DIM, 1)
    values = values.reshape(4, HEAD_DIM, HEAD_DIM).transpose(0, 2, 1).reshape(ROWS, HEAD_DIM)
    pieces = gather_keys(jnp.concatenate([keys, values], axis=0))

    q_own = lax.dynamic_slice_in_dim(query, x_lo * HALF, HALF, 0)
    q_other = x_swap(lax.dynamic_slice_in_dim(query, (1 - x_lo) * HALF, HALF, 0))
    core = jnp.bitwise_and(ctx, 1)
    w_half = x_swap(lax.dynamic_slice_in_dim(out_weight, core * 128, 128, 0))
    w_rest = ctx_permute(w_half, lambda i: i ^ 1)
    w_lower = jnp.where(core == 0, w_half, w_rest)
    w_upper = jnp.where(core == 0, w_rest, w_half)
    w_out = jnp.concatenate([out_weight, w_lower, w_upper], axis=0)
    w_out = lax.dynamic_slice_in_dim(
        jnp.concatenate([w_out, w_out], axis=1), z * (D // Z), D, 1
    )

    bc_here = lax.dynamic_slice_in_dim(w_bc, z * STATE, STATE, 2)
    w_mix = jnp.concatenate(
        [
            w_zx[:, 1],
            bc_here[:, 0],
            bc_here[:, 1],
            jnp.pad(w_dt, ((0, 0), (0, 120))),
            w_zx[:, 0],
        ],
        axis=1,
    )
    w_mix = lax.all_gather(w_mix, "ctx", axis=0, tiled=True)

    context = attend(place, q_own, q_other, pieces)
    attended = sum_over_z(context, w_out)
    residual_here = lax.dynamic_slice(residual, (x_lo * HALF, z * (D // Z)), (HALF, D // Z))
    piece = (residual_here.astype(F32) + attended).astype(BF16)
    near, other = gather_rows(piece)
    own_part = lax.dynamic_slice_in_dim(near[0], x_lo * 256, 256, 1)
    other_part = lax.dynamic_slice_in_dim(other[0], x_lo * 256, 256, 1)
    stream = jnp.where(
        x_lo == 0,
        jnp.concatenate([own_part, other_part], axis=0),
        jnp.concatenate([other_part, own_part], axis=0),
    )
    normed = norm(place, norm_gain[None, :], near, other)

    proj = dot(normed, w_mix[:, : WIDE + 128]).astype(BF16)
    tail = lax.ppermute(proj[ROWS - TAIL :, :WIDE], "ctx", [(i, i + 1) for i in range(15)])
    gate_in = dot(normed, w_mix[:, WIDE + 128 :]).astype(BF16)

    bc_weight = lax.dynamic_slice_in_dim(conv_bc_weight, z * STATE, STATE, 2)
    bc_bias = lax.dynamic_slice_in_dim(conv_bc_bias, z * STATE, STATE, 1)
    taps = jnp.concatenate([conv_x_weight, bc_weight.reshape(CONV, 2 * STATE)], axis=1)
    bias = jnp.concatenate([conv_x_bias, bc_bias.reshape(2 * STATE)])[None, :]
    lanes = ((0, 120),)
    x, bc, cum, step, message = conv_and_state(
        proj, tail, taps, bias, jnp.pad(dt_bias, lanes)[None, :], jnp.pad(a_log, lanes)[None, :]
    )
    state = earlier_state(message, ctx)
    skip = jnp.repeat(d_skip, SSM_HEAD_DIM)[None, :]
    y = local_scan(x, bc, cum, step, skip)
    return stream, finish(y, bc, cum, state, gate_in)


def solution(mesh):
    return jax.shard_map(
        shards,
        mesh=mesh,
        in_specs=(
            P("ctx", "tp"),
            P("ctx", None),
            P("ctx", None),
            P("tp", None),
            P("ctx", None),
            P(),
            P("ctx", None, "tp"),
            P("ctx", None, None),
            P("ctx", "tp"),
            P(None, "tp"),
            P("tp"),
            P(),
            P(),
            P("tp"),
            P("tp"),
            P("tp"),
        ),
        out_specs=(P("ctx", "tp"), P("ctx", "tp")),
        check_vma=False,
    )
```

```python
import functools
import math

import jax
import jax.numpy as jnp
from jax import lax
from jax.experimental import pallas as pl
from jax.experimental.pallas import tpu as pltpu
from jax.sharding import PartitionSpec as P

D = 4096
HEAD_DIM = 128
SSM_HEAD_DIM = 64
STATE = 128
CONV = 4
BLOCK = 128
NEG_BIG = -1e30
EPSILON = 1e-05
HIGHEST = lax.Precision.HIGHEST
F32 = jnp.float32
BF16 = jnp.bfloat16
MIB = 1024 * 1024

Y, Z = 4, 8
ROWS = 512
HALF = 256
TAIL = 16
MSG = STATE + 16


def ctx_permute(block, move):
    return lax.ppermute(block, "ctx", [(i, move(i)) for i in range(16)])


def tp_permute(block, move):
    return lax.ppermute(block, "tp", [(i, move(i)) for i in range(16)])


def y_step(block, d):
    return ctx_permute(block, lambda i: (i + 4 * d) % 16)


def z_step(block, d):
    return tp_permute(block, lambda i: (i + 2 * d) % 16)


def x_swap(block):
    return tp_permute(block, lambda i: i ^ 1)


def dot(a, b, dims=((1,), (0,)), precision=None):
    return lax.dot_general(a, b, (dims, ((), ())), precision=precision, preferred_element_type=F32)


def whole(memory=pltpu.VMEM):
    return pl.BlockSpec(memory_space=memory)


def pack_kernel(place, key, value, out):
    del place
    out[0:ROWS, :] = key[...]
    for j in range(4):
        rows = slice(j * HEAD_DIM, (j + 1) * HEAD_DIM)
        out[ROWS + j * HEAD_DIM : ROWS + (j + 1) * HEAD_DIM, :] = value[rows, :].T


def pack(place, key, value):
    column = pl.BlockSpec((ROWS, HEAD_DIM), lambda i, place: (0, place[2]))
    return pl.pallas_call(
        pack_kernel,
        out_shape=jax.ShapeDtypeStruct((2 * ROWS, HEAD_DIM), BF16),
        grid_spec=pltpu.PrefetchScalarGridSpec(
            num_scalar_prefetch=1,
            grid=(1,),
            in_specs=[column, column],
            out_specs=pl.BlockSpec((2 * ROWS, HEAD_DIM), lambda i, place: (0, 0)),
        ),
        name="pack",
    )(place, key, value)


FIRST = ((0, 0, 0, 0), (0, 1, 0, 1), (3, 0, 0, 2), (1, 0, 0, 3))
SECOND = ((3, 1, 0, 0), (1, 1, 0, 1), (2, 0, 1, 2), (2, 0, 2, 2), (2, 1, 1, 3), (2, 1, 2, 3))


def attend_kernel(homes, last, place, q_own, q_other, *refs):
    count = 2 * len(homes)
    pieces, refs = refs[:count], refs[count:]
    if last:
        (top_in, total_in, acc_in, out), (kv, sems, top, total, acc) = refs[:4], refs[4:]
    else:
        top, total, acc, kv, sems = refs
    me, x_lo = place[0], place[3]
    copies = []
    for i, piece in enumerate(pieces):
        _, _, part, at = homes[i % len(homes)]
        home = kv.at[at + 4 * (i // len(homes))]
        if part:
            home = home.at[pl.ds((part - 1) * ROWS, ROWS)]
        copies.append(pltpu.make_async_copy(piece, home, sems.at[i]))
    for copy in copies:
        copy.start()
    if last:
        top[...] = top_in[...]
        total[...] = total_in[...]
        acc[...] = acc_in[...]
    else:
        top[...] = jnp.full(top.shape, NEG_BIG, F32)
        total[...] = jnp.zeros(total.shape, F32)
        acc[...] = jnp.zeros(acc.shape, F32)
    for copy in copies:
        copy.wait()
    unit = math.log2(math.e) / math.sqrt(HEAD_DIM)

    def block(slot, masked):
        keys = kv[slot, 0:ROWS, :]
        values = jnp.concatenate(
            [kv[slot, ROWS + HEAD_DIM * j : ROWS + HEAD_DIM * (j + 1), :] for j in range(4)], axis=1
        )
        for h in range(4):
            source = q_own if h < 2 else q_other
            queries = source[:, (h % 2) * HEAD_DIM : (h % 2 + 1) * HEAD_DIM]
            scores = dot(keys, queries, ((1,), (1,)))
            if masked:
                key_at = lax.broadcasted_iota(jnp.int32, scores.shape, 0)
                row_at = lax.broadcasted_iota(jnp.int32, scores.shape, 1) + x_lo * HALF
                scores = jnp.where(key_at <= row_at, scores, NEG_BIG)
            old = top[h]
            new = jnp.maximum(old, jnp.max(scores, axis=0, keepdims=True))
            weights = jnp.exp2((scores - new) * unit)
            factor = jnp.exp2((old - new) * unit)
            total[h] = total[h] * factor + jnp.sum(weights, axis=0, keepdims=True)
            acc[h] = acc[h] * factor + dot(values, weights.astype(BF16))
            top[h] = new

    if not last:
        block(0, True)
    places = {at: (apart, crossed) for apart, crossed, _, at in homes}
    aparts = sum(places[at][0] << (2 * at) for at in range(4))
    crosses = sum(places[at][1] << (2 * at) for at in range(4))

    @pl.loop(0 if last else 1, 8)
    def _(slot):
        shift = 2 * jnp.bitwise_and(slot, 3)
        apart = jnp.bitwise_and(lax.shift_right_logical(jnp.int32(aparts), shift), 3)
        crossed = jnp.bitwise_and(lax.shift_right_logical(jnp.int32(crosses), shift), 3)
        y = jnp.bitwise_and(me // 4 + apart, 3)
        rest = jnp.bitwise_xor(jnp.bitwise_and(me, 3), crossed * 2 + slot // 4)

        @pl.when(y * 4 + rest < me)
        def _():
            block(slot, False)

    if last:
        for h in range(4):
            out[:, h * HEAD_DIM : (h + 1) * HEAD_DIM] = (acc[h] / total[h]).T.astype(BF16)


def attend(place, q_own, q_other, pieces, before=None):
    last = before is not None
    state = [
        jax.ShapeDtypeStruct((4, 1, HALF), F32),
        jax.ShapeDtypeStruct((4, 1, HALF), F32),
        jax.ShapeDtypeStruct((4, HEAD_DIM, HALF), F32),
    ]
    scratch = [
        pltpu.VMEM((8, 2 * ROWS, HEAD_DIM), BF16),
        pltpu.SemaphoreType.DMA((len(pieces),)),
    ]
    if last:
        scratch += [pltpu.VMEM(part.shape, part.dtype) for part in state]
    return pl.pallas_call(
        functools.partial(attend_kernel, SECOND if last else FIRST, last),
        out_shape=jax.ShapeDtypeStruct((HALF, 4 * HEAD_DIM), BF16) if last else state,
        in_specs=[whole(pltpu.SMEM), whole(), whole()]
        + [whole(pl.ANY)] * len(pieces)
        + [whole()] * (3 if last else 0),
        out_specs=whole() if last else [whole()] * 3,
        scratch_shapes=scratch,
        compiler_params=pltpu.CompilerParams(vmem_limit_bytes=32 * MIB),
        cost_estimate=pl.CostEstimate(
            flops=2_200_000_000, bytes_accessed=5_000_000, transcendentals=4_200_000
        ),
        name="attend_rest" if last else "attend_first",
    )(place, q_own, q_other, *pieces, *(before or ()))


def project_kernel(place, context, w_own, w_half, w_rest, *refs):
    parts, weight = refs[:9], refs[9]
    core, z = jnp.bitwise_and(place[0], 1), place[2]
    weight[0:HALF, :] = w_own[...]
    weight[pl.ds(pl.multiple_of(HALF + core * 128, 128), 128), :] = w_half[...]
    weight[pl.ds(pl.multiple_of(HALF + (1 - core) * 128, 128), 128), :] = w_rest[...]
    wide = D // Z
    for k in range(Z):
        column = pl.multiple_of(jnp.bitwise_and(z + k, Z - 1) * wide, wide)
        part = dot(context[...], weight[:, pl.ds(column, wide)]).astype(BF16)
        if k == 4:
            parts[4][...] = part[:, : wide // 2]
            parts[8][...] = part[:, wide // 2 :]
        else:
            parts[k][...] = part


def project(place, context, weights):
    wide = D // Z
    out = [jax.ShapeDtypeStruct((HALF, wide // 2 if k in (4, 8) else wide), BF16) for k in range(9)]
    return pl.pallas_call(
        project_kernel,
        out_shape=out,
        in_specs=[whole(pltpu.SMEM)] + [whole()] * 4,
        out_specs=[whole()] * 9,
        scratch_shapes=[pltpu.VMEM((ROWS, D), BF16)],
        compiler_params=pltpu.CompilerParams(vmem_limit_bytes=32 * MIB),
        cost_estimate=pl.CostEstimate(
            flops=1_100_000_000, bytes_accessed=6_500_000, transcendentals=0
        ),
        name="project",
    )(place, context, *weights)


def sum_over_z(parts):
    half = parts[4].shape[1]
    up, down = z_step(parts[4], 1), z_step(parts[8], -1)
    third, fifth = parts[3].astype(F32), parts[5].astype(F32)
    up = jnp.concatenate([third[:, :half] + up.astype(F32), third[:, half:]], axis=1)
    down = jnp.concatenate([fifth[:, :half], fifth[:, half:] + down.astype(F32)], axis=1)
    for k in (2, 1, 0):
        up, down = lax.optimization_barrier((up.astype(BF16), down.astype(BF16)))
        up, down = z_step(up, 1), z_step(down, -1)
        if k:
            up = parts[k].astype(F32) + up.astype(F32)
            down = parts[8 - k].astype(F32) + down.astype(F32)
    return parts[0].astype(F32) + up.astype(F32) + down.astype(F32)


MIXED = 1408


def mix_kernel(steps, first, last, place, gain, weights, *refs):
    count = sum(len(sources) for _, _, sources in steps)
    blocks, refs = refs[:count], refs[count:]
    if not first:
        (square_in, acc_in), refs = refs[:2], refs[2:]
    (square, acc), (held, sems) = refs[:2], refs[2:4]
    if last:
        total, squares = refs[4], refs[5]
    else:
        total, squares = acc, square
    z, x_lo = place[2], place[3]
    wide = D // Z
    apart = []
    for k, _, _ in steps:
        if k not in apart:
            apart.append(k)
    starts = [pl.multiple_of(jnp.bitwise_and(z + k, Z - 1) * wide, wide) for k in apart]
    copies = [
        pltpu.make_async_copy(weights.at[pl.ds(start, wide)], held.at[i], sems.at[i])
        for i, start in enumerate(starts)
    ]
    for copy in copies:
        copy.start()
    if first:
        squares[...] = jnp.zeros(squares.shape, F32)
        total[...] = jnp.zeros(total.shape, F32)
    else:
        squares[...] = square_in[...]
        total[...] = acc_in[...]
    done = 0
    waited = set()
    for k, own, sources in steps:
        i = apart.index(k)
        if k not in waited:
            waited.add(k)
            copies[i].wait()
        rows = pl.ds(pl.multiple_of((x_lo if own else 1 - x_lo) * HALF, HALF), HALF)
        parts = [blocks[done + j][...] for j in range(len(sources))]
        done += len(sources)
        value = (jnp.concatenate(parts, axis=1) if len(parts) > 1 else parts[0]).astype(F32)
        square_sum = value * value
        squares[rows, :] += sum(square_sum[:, j * 128 : (j + 1) * 128] for j in range(wide // 128))
        scaled = (value * gain[:, pl.ds(starts[i], wide)]).astype(BF16)
        total[rows, :] += dot(scaled, held[i])
    if last:
        proj, gate = square, acc
        mean = jnp.sum(squares[...], axis=1, keepdims=True) * (1.0 / D)
        result = (total[...] * lax.rsqrt(mean + EPSILON)).astype(BF16)
        proj[...] = result[:, : MIXED - INNER]
        gate[...] = result[:, MIXED - INNER :]


def mix(place, gain, weights, steps, before=None, last=False):
    blocks = [block for _, _, sources in steps for block in sources]
    apart = len({k for k, _, _ in steps})
    sums = [(ROWS, 128), (ROWS, MIXED)]
    if last:
        out = [
            jax.ShapeDtypeStruct((ROWS, MIXED - INNER), BF16),
            jax.ShapeDtypeStruct((ROWS, INNER), BF16),
        ]
    else:
        out = [jax.ShapeDtypeStruct(shape, F32) for shape in sums]
    scratch = [
        pltpu.VMEM((apart, D // Z, MIXED), BF16),
        pltpu.SemaphoreType.DMA((apart,)),
    ]
    if last:
        scratch += [pltpu.VMEM(sums[1], F32), pltpu.VMEM(sums[0], F32)]
    flops = 2 * HALF * (D // Z) * MIXED * len(steps)
    return pl.pallas_call(
        functools.partial(mix_kernel, steps_only(steps), before is None, last),
        out_shape=out,
        in_specs=[whole(pltpu.SMEM), whole(), whole(pl.ANY)]
        + [whole()] * (len(blocks) + (0 if before is None else 2)),
        out_specs=[whole()] * 2,
        scratch_shapes=scratch,
        compiler_params=pltpu.CompilerParams(vmem_limit_bytes=40 * MIB),
        cost_estimate=pl.CostEstimate(
            flops=flops, bytes_accessed=1_500_000 * apart + 6_000_000, transcendentals=0
        ),
        name="mix_last" if last else "mix",
    )(place, gain, weights, *blocks, *(before or ()))


def steps_only(steps):
    return tuple((k, own, tuple(range(len(sources)))) for k, own, sources in steps)


def project_stream(place, gain, weights, piece):
    half = piece.shape[1] // 2
    tie = lax.optimization_barrier

    def left(block):
        return block[:, :half]

    def right(block):
        return block[:, half:]

    near, other_l, other_r = {0: piece}, {}, {}
    near[7], near[1], other_0 = tie((z_step(piece, 1), z_step(piece, -1), x_swap(piece)))
    other_l[0], other_r[0] = left(other_0), right(other_0)
    for k in (1, 2):
        got = (
            z_step(near[8 - k], 1),
            z_step(near[k], -1),
            z_step(other_l[(9 - k) % 8], 1),
            z_step(other_l[k - 1], -1),
            x_swap(right(near[8 - k])),
            x_swap(right(near[k])),
        )
        near[7 - k], near[k + 1], other_l[8 - k], other_l[k], other_r[8 - k], other_r[k] = tie(got)
    early = [(0, True, (piece,)), (0, False, (other_0,))]
    for k in (7, 1):
        early += [(k, True, (near[k],)), (k, False, (other_l[k], other_r[k]))]
    for k in (6, 2):
        early += [(k, True, (near[k],))]
    sums = mix(place, gain, weights, early)
    got = (
        z_step(left(near[5]), 1),
        z_step(right(near[3]), -1),
        z_step(other_l[6], 1),
        z_step(other_l[2], -1),
        x_swap(right(near[5])),
        x_swap(right(near[3])),
        sums,
    )
    far_l, far_r, other_l[5], other_l[3], other_r[5], other_r[3], sums = tie(got)
    other_l[4], other_r[4] = z_step(other_l[5], 1), x_swap(far_r)
    late = [(k, True, (near[k],)) for k in (5, 3)] + [(4, True, (far_l, far_r))]
    late += [(k, False, (other_l[k], other_r[k])) for k in (6, 2, 5, 3)]
    sums = mix(place, gain, weights, late, sums)
    return mix(place, gain, weights, [(4, False, (other_l[4], other_r[4]))], sums, last=True)


INNER = 512
WIDE = INNER + 2 * STATE


def silu(values):
    return values / (1.0 + jnp.exp(-values))


def per_channel(values):
    head = lax.broadcasted_iota(jnp.int32, (128, INNER), 0)
    channel = lax.broadcasted_iota(jnp.int32, (128, INNER), 1)
    spread = (head == channel // SSM_HEAD_DIM).astype(BF16)
    return dot(values.astype(BF16), spread)


def conv_kernel(proj, tail, weight, bias, dt_bias, a_log, x_out, bc_out, cum_out, dt_out, msg, pad):
    pad[0:TAIL, :] = tail[...].astype(F32)
    pad[TAIL:, :] = proj[:, 0:WIDE].astype(F32)
    summed = bias[...] + weight[0:1, :] * pad[pl.ds(TAIL - CONV + 1, ROWS), :]
    for k in range(1, CONV):
        summed = summed + weight[k : k + 1, :] * pad[pl.ds(TAIL - CONV + 1 + k, ROWS), :]
    conv = silu(summed).astype(BF16)
    x_out[...] = conv[:, :INNER]
    bc_out[...] = conv[:, INNER:]
    raw = proj[:, WIDE:].astype(F32) + dt_bias[...]
    step = jnp.maximum(raw, 0.0) + jnp.log1p(jnp.exp(-jnp.abs(raw)))
    dt_out[...] = step
    rate = -jnp.exp(a_log[...]) * step
    later = lax.broadcasted_iota(jnp.int32, (BLOCK, BLOCK), 0)
    earlier = lax.broadcasted_iota(jnp.int32, (BLOCK, BLOCK), 1)
    lower = (later >= earlier).astype(F32)
    base = jnp.zeros((1, 128), F32)
    for k in range(ROWS // BLOCK):
        rows = slice(k * BLOCK, (k + 1) * BLOCK)
        here = dot(lower, rate[rows], precision=HIGHEST) + base
        cum_out[rows, :] = here
        base = here[BLOCK - 1 : BLOCK, :]
    left = step * jnp.exp(base - cum_out[...])
    weighted = (x_out[...].astype(F32) * per_channel(left)).astype(BF16)
    msg[0:STATE, :] = dot(bc_out[:, :STATE], weighted, ((0,), (0,))).astype(BF16)
    msg[STATE:, :] = per_channel(jnp.broadcast_to(jnp.exp(base), (16, 128))).astype(BF16)


def conv_and_state(proj, tail, weight, bias, dt_bias, a_log):
    return pl.pallas_call(
        conv_kernel,
        out_shape=(
            jax.ShapeDtypeStruct((ROWS, INNER), BF16),
            jax.ShapeDtypeStruct((ROWS, 2 * STATE), BF16),
            jax.ShapeDtypeStruct((ROWS, 128), F32),
            jax.ShapeDtypeStruct((ROWS, 128), F32),
            jax.ShapeDtypeStruct((MSG, INNER), BF16),
        ),
        in_specs=[whole()] * 6,
        out_specs=(whole(),) * 5,
        scratch_shapes=[pltpu.VMEM((ROWS + TAIL, WIDE), F32)],
        compiler_params=pltpu.CompilerParams(vmem_limit_bytes=32 * MIB),
        cost_estimate=pl.CostEstimate(
            flops=200_000_000, bytes_accessed=3_000_000, transcendentals=800_000
        ),
        name="conv_and_state",
    )(proj, tail, weight, bias, dt_bias, a_log)


def scan_kernel(x_ref, bc, cum, step, d_skip, out):
    lower = lax.broadcasted_iota(jnp.int32, (BLOCK, BLOCK), 0) >= lax.broadcasted_iota(
        jnp.int32, (BLOCK, BLOCK), 1
    )
    low_lane = lax.broadcasted_iota(jnp.int32, (BLOCK, 128), 1) < SSM_HEAD_DIM
    state = None
    for k in range(ROWS // BLOCK):
        rows = slice(k * BLOCK, (k + 1) * BLOCK)
        b, c = bc[rows, :STATE], bc[rows, STATE:]
        x = x_ref[rows, :]
        here = cum[rows, :]
        here_t, step_t = here.T, step[rows, :].T
        met = jnp.where(lower, dot(c, b, ((1,), (1,))), 0.0)
        parts = []
        for pair in range(4):
            left = []
            for h in (2 * pair, 2 * pair + 1):
                gap = jnp.minimum(here[:, h : h + 1] - here_t[h : h + 1, :], 0.0)
                left.append((met * jnp.exp(gap) * step_t[h : h + 1, :]).astype(BF16))
            xs = x[:, pair * 128 : (pair + 1) * 128]
            none = jnp.zeros_like(xs)
            right = jnp.concatenate([jnp.where(low_lane, xs, none), jnp.where(low_lane, none, xs)], 0)
            parts.append(dot(jnp.concatenate(left, axis=1), right))
        y = jnp.concatenate(parts, axis=1)
        last = here[BLOCK - 1 : BLOCK, :]
        if k:
            start = cum[k * BLOCK - 1 : k * BLOCK, :]
            y = y + dot(c, state.astype(BF16)) * per_channel(jnp.exp(here - start))
        out[rows, :] = y + d_skip[...] * x.astype(F32)
        if k < ROWS // BLOCK - 1:
            weighted = per_channel(step[rows, :] * jnp.exp(last - here)) * x.astype(F32)
            added = dot(b, weighted.astype(BF16), ((0,), (0,)))
            if k:
                kept = per_channel(jnp.broadcast_to(jnp.exp(last - start), (8, 128)))[0:1, :]
                state = state * kept + added
            else:
                state = added


def local_scan(x, bc, cum, step, d_skip):
    return pl.pallas_call(
        scan_kernel,
        out_shape=jax.ShapeDtypeStruct((ROWS, INNER), F32),
        in_specs=[whole()] * 5,
        out_specs=whole(),
        compiler_params=pltpu.CompilerParams(vmem_limit_bytes=32 * MIB),
        cost_estimate=pl.CostEstimate(
            flops=400_000_000, bytes_accessed=3_000_000, transcendentals=600_000
        ),
        name="local_scan",
    )(x, bc, cum, step, d_skip)


def gate_kernel(y, bc, cum, state, gate, out):
    carried = dot(bc[:, STATE:], state[...]) * per_channel(jnp.exp(cum[...]))
    out[...] = ((y[...] + carried) * silu(gate[...].astype(F32))).astype(BF16)


def finish(y, bc, cum, state, gate):
    return pl.pallas_call(
        gate_kernel,
        out_shape=jax.ShapeDtypeStruct((ROWS, INNER), BF16),
        in_specs=[whole()] * 5,
        out_specs=whole(),
        compiler_params=pltpu.CompilerParams(vmem_limit_bytes=32 * MIB),
        cost_estimate=pl.CostEstimate(
            flops=70_000_000, bytes_accessed=3_500_000, transcendentals=600_000
        ),
        name="gate",
    )(y, bc, cum, state, gate)


def then(earlier, later):
    return (earlier[0] * later[1] + later[0], earlier[1] * later[1])


def unpack(message):
    values = message.astype(F32)
    return values[:STATE], values[STATE : STATE + 1]


def earlier_state(message, ctx):
    position = jnp.bitwise_and(ctx, 3)
    met = [message] + [ctx_permute(message, lambda i, d=d: i ^ d) for d in (1, 2, 3)]
    met = [unpack(part) for part in met]
    none = (jnp.zeros((STATE, INNER), F32), jnp.ones((1, INNER), F32))
    before, block = none, none
    for p in range(4):
        apart = jnp.bitwise_xor(position, p)
        part = tuple(
            jnp.where(apart == 0, a, jnp.where(apart == 1, b, jnp.where(apart == 2, c, d)))
            for a, b, c, d in zip(*met)
        )
        follow = then(before, part)
        before = tuple(jnp.where(p < position, a, b) for a, b in zip(follow, before))
        block = then(block, part)
    packed = jnp.concatenate([block[0], jnp.broadcast_to(block[1], (16, INNER))]).astype(BF16)
    blocks = []
    for d in (1, 2, 3):
        pairs = [(i, i + 4 * d) for i in range(16) if i + 4 * d < 16]
        blocks.append(unpack(lax.ppermute(packed, "ctx", pairs)))
    near, mid, far = blocks
    incoming = then(then(far, mid), near)[0]
    return (incoming * before[1] + before[0]).astype(BF16)


def shards(
    query,
    key,
    value,
    out_weight,
    residual,
    norm_gain,
    w_zx,
    w_bc,
    w_dt,
    conv_x_weight,
    conv_x_bias,
    conv_bc_weight,
    conv_bc_bias,
    dt_bias,
    a_log,
    d_skip,
):
    tp, ctx = lax.axis_index("tp"), lax.axis_index("ctx")
    z, x_lo = tp // 2, jnp.bitwise_and(tp, 1)
    place = jnp.stack([ctx, x_lo * HALF, z, x_lo]).astype(jnp.int32)

    core = jnp.bitwise_and(ctx, 1)
    tie = lax.optimization_barrier
    mine = pack(place, key, value)
    mine, w_zx, w_bc, w_dt, query, w_send = tie((mine, w_zx, w_bc, w_dt, query, out_weight))
    across = ctx_permute(mine, lambda i: i ^ 2)
    below, above = y_step(mine, 1), y_step(mine, -1)
    bc_here = lax.dynamic_slice_in_dim(w_bc, z * STATE, STATE, 2)
    w_mix = jnp.concatenate(
        [
            w_zx[:, 1],
            bc_here[:, 0],
            bc_here[:, 1],
            jnp.pad(w_dt, ((0, 0), (0, 120))),
            w_zx[:, 0],
        ],
        axis=1,
    )
    q_own = lax.dynamic_slice_in_dim(query, x_lo * HALF, HALF, 0)
    q_send = lax.dynamic_slice_in_dim(query, (1 - x_lo) * HALF, HALF, 0)
    w_send = lax.dynamic_slice_in_dim(w_send, core * 128, 128, 0)
    across, below, above, q_send, w_send, w_mix = tie((across, below, above, q_send, w_send, w_mix))
    below_x, above_x = y_step(across, 1), y_step(across, -1)
    far = y_step(below[:ROWS], 1), y_step(above[ROWS:], -1)
    q_other = x_swap(q_send)
    w_half = x_swap(w_send)
    held = [mine, across, below, above]
    held += [ctx_permute(part, lambda i: i ^ 1) for part in held]
    state = attend(place, q_own, q_other, held)
    below_x, above_x, far, w_mix, state = tie((below_x, above_x, far, w_mix, state))
    w_mix = lax.all_gather(w_mix, "ctx", axis=0, tiled=True)
    far_x = y_step(below_x[:ROWS], 1), y_step(above_x[ROWS:], -1)
    late = [below_x, above_x, *far, *far_x]
    late += [ctx_permute(part, lambda i: i ^ 1) for part in late]
    state, late, w_half = tie((state, late, w_half))
    w_rest = ctx_permute(w_half, lambda i: i ^ 1)
    context = attend(place, q_own, q_other, late, state)
    parts = project(place, context, (out_weight, w_half, w_rest))
    attended = sum_over_z(parts)
    residual_here = lax.dynamic_slice(residual, (x_lo * HALF, z * (D // Z)), (HALF, D // Z))
    piece = (residual_here.astype(F32) + attended).astype(BF16)
    stream_own = lax.dynamic_slice_in_dim(piece, x_lo * 256, 256, 1)
    stream_other = x_swap(lax.dynamic_slice_in_dim(piece, (1 - x_lo) * 256, 256, 1))
    stream = jnp.where(
        x_lo == 0,
        jnp.concatenate([stream_own, stream_other], axis=0),
        jnp.concatenate([stream_other, stream_own], axis=0),
    )
    proj, gate_in = project_stream(place, norm_gain[None, :], w_mix, piece)
    tail = lax.ppermute(proj[ROWS - TAIL :, :WIDE], "ctx", [(i, i + 1) for i in range(15)])

    bc_weight = lax.dynamic_slice_in_dim(conv_bc_weight, z * STATE, STATE, 2)
    bc_bias = lax.dynamic_slice_in_dim(conv_bc_bias, z * STATE, STATE, 1)
    taps = jnp.concatenate([conv_x_weight, bc_weight.reshape(CONV, 2 * STATE)], axis=1)
    bias = jnp.concatenate([conv_x_bias, bc_bias.reshape(2 * STATE)])[None, :]
    lanes = ((0, 120),)
    x, bc, cum, step, message = conv_and_state(
        proj, tail, taps, bias, jnp.pad(dt_bias, lanes)[None, :], jnp.pad(a_log, lanes)[None, :]
    )
    state = earlier_state(message, ctx)
    skip = jnp.repeat(d_skip, SSM_HEAD_DIM)[None, :]
    y = local_scan(x, bc, cum, step, skip)
    return stream, finish(y, bc, cum, state, gate_in)


def solution(mesh):
    return jax.shard_map(
        shards,
        mesh=mesh,
        in_specs=(
            P("ctx", "tp"),
            P("ctx", None),
            P("ctx", None),
            P("tp", None),
            P("ctx", None),
            P(),
            P("ctx", None, "tp"),
            P("ctx", None, None),
            P("ctx", "tp"),
            P(None, "tp"),
            P("tp"),
            P(),
            P(),
            P("tp"),
            P("tp"),
            P("tp"),
        ),
        out_specs=(P("ctx", "tp"), P("ctx", "tp")),
        check_vma=False,
    )
```

```python
import functools
import math

import jax
import jax.numpy as jnp
from jax import lax
from jax.experimental import pallas as pl
from jax.experimental.pallas import tpu as pltpu
from jax.sharding import PartitionSpec as P

D = 4096
HEAD_DIM = 128
SSM_HEAD_DIM = 64
STATE = 128
CONV = 4
BLOCK = 128
NEG_BIG = -1e30
EPSILON = 1e-05
HIGHEST = lax.Precision.HIGHEST
F32 = jnp.float32
BF16 = jnp.bfloat16
MIB = 1024 * 1024

Y, Z = 4, 8
ROWS = 512
HALF = 256
EARLY = 96
TAIL = 16
MSG = STATE + 16


def ctx_permute(block, move):
    return lax.ppermute(block, "ctx", [(i, move(i)) for i in range(16)])


def tp_permute(block, move):
    return lax.ppermute(block, "tp", [(i, move(i)) for i in range(16)])


def y_step(block, d):
    return ctx_permute(block, lambda i: (i + 4 * d) % 16)


def z_step(block, d):
    return tp_permute(block, lambda i: (i + 2 * d) % 16)


def x_swap(block):
    return tp_permute(block, lambda i: i ^ 1)


def dot(a, b, dims=((1,), (0,)), precision=None):
    return lax.dot_general(a, b, (dims, ((), ())), precision=precision, preferred_element_type=F32)


def whole(memory=pltpu.VMEM):
    return pl.BlockSpec(memory_space=memory)


def pack_kernel(place, key, value, out):
    del place
    out[0:ROWS, :] = key[...]
    for j in range(4):
        rows = slice(j * HEAD_DIM, (j + 1) * HEAD_DIM)
        out[ROWS + j * HEAD_DIM : ROWS + (j + 1) * HEAD_DIM, :] = value[rows, :].T


def pack(place, key, value):
    column = pl.BlockSpec((ROWS, HEAD_DIM), lambda i, place: (0, place[2]))
    return pl.pallas_call(
        pack_kernel,
        out_shape=jax.ShapeDtypeStruct((2 * ROWS, HEAD_DIM), BF16),
        grid_spec=pltpu.PrefetchScalarGridSpec(
            num_scalar_prefetch=1,
            grid=(1,),
            in_specs=[column, column],
            out_specs=pl.BlockSpec((2 * ROWS, HEAD_DIM), lambda i, place: (0, 0)),
        ),
        name="pack",
    )(place, key, value)


FIRST = ((0, 0, 0, 0), (0, 1, 0, 1), (3, 0, 0, 2), (1, 0, 0, 3))
SECOND = ((3, 1, 0, 0), (1, 1, 0, 1), (2, 0, 1, 2), (2, 0, 2, 2), (2, 1, 1, 3), (2, 1, 2, 3))


def attend_kernel(homes, last, place, q_own, q_other, *refs):
    count = 2 * len(homes)
    pieces, refs = refs[:count], refs[count:]
    if last:
        (top_in, total_in, acc_in, out), (kv, sems, top, total, acc) = refs[:4], refs[4:]
    else:
        top, total, acc, kv, sems = refs
    me, x_lo = place[0], place[3]
    copies = []
    for i, piece in enumerate(pieces):
        _, _, part, at = homes[i % len(homes)]
        home = kv.at[at + 4 * (i // len(homes))]
        if part:
            home = home.at[pl.ds((part - 1) * ROWS, ROWS)]
        copies.append(pltpu.make_async_copy(piece, home, sems.at[i]))
    for copy in copies:
        copy.start()
    if last:
        top[...] = top_in[...]
        total[...] = total_in[...]
        acc[...] = acc_in[...]
    else:
        top[...] = jnp.full(top.shape, NEG_BIG, F32)
        total[...] = jnp.zeros(total.shape, F32)
        acc[...] = jnp.zeros(acc.shape, F32)
    for copy in copies:
        copy.wait()
    unit = math.log2(math.e) / math.sqrt(HEAD_DIM)

    def block(slot, masked):
        keys = kv[slot, 0:ROWS, :]
        values = jnp.concatenate(
            [kv[slot, ROWS + HEAD_DIM * j : ROWS + HEAD_DIM * (j + 1), :] for j in range(4)], axis=1
        )
        heads = range(4)
        scores = []
        for h in heads:
            source = q_own if h < 2 else q_other
            queries = source[:, (h % 2) * HEAD_DIM : (h % 2 + 1) * HEAD_DIM]
            scores.append(dot(keys, queries, ((1,), (1,))))
        if masked:
            key_at = lax.broadcasted_iota(jnp.int32, scores[0].shape, 0)
            row_at = lax.broadcasted_iota(jnp.int32, scores[0].shape, 1) + x_lo * HALF
            visible = key_at <= row_at
            scores = [jnp.where(visible, score, NEG_BIG) for score in scores]
        old = [top[h] for h in heads]
        new = [jnp.maximum(old[h], jnp.max(scores[h], axis=0, keepdims=True)) for h in heads]
        weights = [jnp.exp2((scores[h] - new[h]) * unit) for h in heads]
        factor = [jnp.exp2((old[h] - new[h]) * unit) for h in heads]
        sums = [jnp.sum(weights[h], axis=0, keepdims=True) for h in heads]
        mixed = [dot(values, weights[h].astype(BF16)) for h in heads]
        for h in heads:
            total[h] = total[h] * factor[h] + sums[h]
            acc[h] = acc[h] * factor[h] + mixed[h]
            top[h] = new[h]

    if not last:
        block(0, True)
    places = {at: (apart, crossed) for apart, crossed, _, at in homes}
    aparts = sum(places[at][0] << (2 * at) for at in range(4))
    crosses = sum(places[at][1] << (2 * at) for at in range(4))

    @pl.loop(0 if last else 1, 8)
    def _(slot):
        shift = 2 * jnp.bitwise_and(slot, 3)
        apart = jnp.bitwise_and(lax.shift_right_logical(jnp.int32(aparts), shift), 3)
        crossed = jnp.bitwise_and(lax.shift_right_logical(jnp.int32(crosses), shift), 3)
        y = jnp.bitwise_and(me // 4 + apart, 3)
        rest = jnp.bitwise_xor(jnp.bitwise_and(me, 3), crossed * 2 + slot // 4)

        @pl.when(y * 4 + rest < me)
        def _():
            block(slot, False)

    if last:
        for h in range(4):
            out[:, h * HEAD_DIM : (h + 1) * HEAD_DIM] = (acc[h] / total[h]).T.astype(BF16)


def attend(place, q_own, q_other, pieces, before=None):
    last = before is not None
    state = [
        jax.ShapeDtypeStruct((4, 1, HALF), F32),
        jax.ShapeDtypeStruct((4, 1, HALF), F32),
        jax.ShapeDtypeStruct((4, HEAD_DIM, HALF), F32),
    ]
    scratch = [
        pltpu.VMEM((8, 2 * ROWS, HEAD_DIM), BF16),
        pltpu.SemaphoreType.DMA((12,)),
    ]
    if last:
        scratch += [pltpu.VMEM(part.shape, part.dtype) for part in state]
    return pl.pallas_call(
        functools.partial(attend_kernel, SECOND if last else FIRST, last),
        out_shape=jax.ShapeDtypeStruct((HALF, 4 * HEAD_DIM), BF16) if last else state,
        in_specs=[whole(pltpu.SMEM), whole(), whole()]
        + [whole(pl.ANY)] * len(pieces)
        + [whole()] * (3 if last else 0),
        out_specs=whole() if last else [whole()] * 3,
        scratch_shapes=scratch,
        compiler_params=pltpu.CompilerParams(vmem_limit_bytes=32 * MIB),
        cost_estimate=pl.CostEstimate(
            flops=1_000_000, bytes_accessed=1_000_000, transcendentals=0
        ),
        name="attend_rest" if last else "attend_first",
    )(place, q_own, q_other, *pieces, *(before or ()))


def project_kernel(place, context, w_own, half_0, half_1, rest_0, rest_1, *refs):
    parts, weight = refs[:9], refs[9]
    core, z = jnp.bitwise_and(place[0], 1), place[2]
    weight[0:HALF, :] = w_own[...]
    for first, second, which in ((half_0, half_1, core), (rest_0, rest_1, 1 - core)):
        start = pl.multiple_of(HALF + which * 128, 128)
        weight[pl.ds(start, EARLY), :] = first[...]
        weight[pl.ds(start + EARLY, 128 - EARLY), :] = second[...]
    wide = D // Z
    for k in range(Z):
        column = pl.multiple_of(jnp.bitwise_and(z + k, Z - 1) * wide, wide)
        part = dot(context[...], weight[:, pl.ds(column, wide)]).astype(BF16)
        if k == 4:
            parts[4][...] = part[:, : wide // 2]
            parts[8][...] = part[:, wide // 2 :]
        else:
            parts[k][...] = part


def project(place, context, weights):
    wide = D // Z
    out = [jax.ShapeDtypeStruct((HALF, wide // 2 if k in (4, 8) else wide), BF16) for k in range(9)]
    return pl.pallas_call(
        project_kernel,
        out_shape=out,
        in_specs=[whole(pltpu.SMEM)] + [whole()] * 6,
        out_specs=[whole()] * 9,
        scratch_shapes=[pltpu.VMEM((ROWS, D), BF16)],
        compiler_params=pltpu.CompilerParams(vmem_limit_bytes=32 * MIB),
        cost_estimate=pl.CostEstimate(
            flops=1_100_000_000, bytes_accessed=6_500_000, transcendentals=0
        ),
        name="project",
    )(place, context, *weights)


def sum_over_z(parts):
    half = parts[4].shape[1]
    up, down = z_step(parts[4], 1), z_step(parts[8], -1)
    third, fifth = parts[3].astype(F32), parts[5].astype(F32)
    up = jnp.concatenate([third[:, :half] + up.astype(F32), third[:, half:]], axis=1)
    down = jnp.concatenate([fifth[:, :half], fifth[:, half:] + down.astype(F32)], axis=1)
    for k in (2, 1, 0):
        up, down = lax.optimization_barrier((up.astype(BF16), down.astype(BF16)))
        up, down = z_step(up, 1), z_step(down, -1)
        if k:
            up = parts[k].astype(F32) + up.astype(F32)
            down = parts[8 - k].astype(F32) + down.astype(F32)
    return parts[0].astype(F32) + up.astype(F32) + down.astype(F32)


MIXED = 1408


def mix_kernel(steps, first, last, place, gain, weights, *refs):
    count = 1 + max(array for _, _, sources in steps for array, _, _ in sources)
    blocks, refs = refs[:count], refs[count:]
    if not first:
        (square_in, acc_in), refs = refs[:2], refs[2:]
    (square, acc), (held, sems) = refs[:2], refs[2:4]
    if last:
        total, squares = refs[4], refs[5]
    else:
        total, squares = acc, square
    z, x_lo = place[2], place[3]
    wide = D // Z
    apart = []
    for k, _, _ in steps:
        if k not in apart:
            apart.append(k)
    starts = [pl.multiple_of(jnp.bitwise_and(z + k, Z - 1) * wide, wide) for k in apart]
    copies = [
        pltpu.make_async_copy(weights.at[pl.ds(start, wide)], held.at[i], sems.at[i])
        for i, start in enumerate(starts)
    ]
    for copy in copies:
        copy.start()
    if first:
        squares[...] = jnp.zeros(squares.shape, F32)
        total[...] = jnp.zeros(total.shape, F32)
    else:
        squares[...] = square_in[...]
        total[...] = acc_in[...]
    waited = set()
    for k, own, sources in steps:
        i = apart.index(k)
        if k not in waited:
            waited.add(k)
            copies[i].wait()
        rows = pl.ds(pl.multiple_of((x_lo if own else 1 - x_lo) * HALF, HALF), HALF)
        parts = [blocks[array][:, at : at + width] for array, at, width in sources]
        value = (jnp.concatenate(parts, axis=1) if len(parts) > 1 else parts[0]).astype(F32)
        square_sum = value * value
        squares[rows, :] += sum(square_sum[:, j * 128 : (j + 1) * 128] for j in range(wide // 128))
        scaled = (value * gain[:, pl.ds(starts[i], wide)]).astype(BF16)
        total[rows, :] += dot(scaled, held[i])
    if last:
        proj, gate = square, acc
        mean = jnp.sum(squares[...], axis=1, keepdims=True) * (1.0 / D)
        result = (total[...] * lax.rsqrt(mean + EPSILON)).astype(BF16)
        proj[...] = result[:, : MIXED - INNER]
        gate[...] = result[:, MIXED - INNER :]


def mix(place, gain, weights, steps, before=None, last=False):
    blocks, plan = [], []
    for k, own, sources in steps:
        found = []
        for array, at, width in sources:
            known = [i for i, block in enumerate(blocks) if block is array]
            if not known:
                known = [len(blocks)]
                blocks.append(array)
            found.append((known[0], at, width))
        plan.append((k, own, tuple(found)))
    apart = len({k for k, _, _ in steps})
    sums = [(ROWS, 128), (ROWS, MIXED)]
    if last:
        out = [
            jax.ShapeDtypeStruct((ROWS, MIXED - INNER), BF16),
            jax.ShapeDtypeStruct((ROWS, INNER), BF16),
        ]
    else:
        out = [jax.ShapeDtypeStruct(shape, F32) for shape in sums]
    scratch = [
        pltpu.VMEM((apart, D // Z, MIXED), BF16),
        pltpu.SemaphoreType.DMA((apart,)),
    ]
    if last:
        scratch += [pltpu.VMEM(sums[1], F32), pltpu.VMEM(sums[0], F32)]
    flops = 2 * HALF * (D // Z) * MIXED * len(steps)
    return pl.pallas_call(
        functools.partial(mix_kernel, tuple(plan), before is None, last),
        out_shape=out,
        in_specs=[whole(pltpu.SMEM), whole(), whole(pl.ANY)]
        + [whole()] * (len(blocks) + (0 if before is None else 2)),
        out_specs=[whole()] * 2,
        scratch_shapes=scratch,
        compiler_params=pltpu.CompilerParams(vmem_limit_bytes=40 * MIB),
        cost_estimate=pl.CostEstimate(
            flops=flops, bytes_accessed=1_500_000 * apart + 6_000_000, transcendentals=0
        ),
        name="mix_last" if last else "mix",
    )(place, gain, weights, *blocks, *(before or ()))


def project_stream(place, gain, weights, piece):
    wide = piece.shape[1]
    half = wide // 2
    tie = lax.optimization_barrier

    def joined(*blocks):
        return jnp.concatenate(blocks, axis=1)

    up, down, other_0 = tie((z_step(piece, 1), z_step(piece, -1), x_swap(piece)))
    left = other_0[:, :half]
    near_up, near_down = (up, 0), (down, 0)
    up, down = joined(up, left), joined(left, down)
    near = {0: ((piece, 0, wide),), 7: ((*near_up, wide),), 1: ((*near_down, wide),)}
    other = {0: ((other_0, 0, wide),)}
    sums = None
    for k in (1, 2):
        right = joined(up[:, half:wide], down[:, wide:])
        got = (z_step(up, 1), z_step(down, -1), x_swap(right))
        if k == 2:
            early = [(0, True, near[0]), (0, False, other[0])]
            early += [(j, own, from_[j]) for j in (7, 1) for own, from_ in ((True, near), (False, other))]
            early += [(j, True, near[j]) for j in (6, 2)]
            got = tie((*got, *mix(place, gain, weights, early)))
            got, sums = got[:3], got[3:]
        else:
            got = tie(got)
        up, down, right = got
        near[7 - k], near[k + 1] = ((up, 0, wide),), ((down, half, wide),)
        other[8 - k] = (up, wide, half), (right, 0, half)
        other[k] = (down, 0, half), (right, half, half)
    middle = [(k, True, near[k]) for k in (5, 3)] + [(k, False, other[k]) for k in (6, 2)]
    right = joined(up[:, half:wide], down[:, wide:])
    up, down, right, sums = tie(
        (
            z_step(up[:, half:], 1),
            z_step(down[:, :wide], -1),
            x_swap(right),
            mix(place, gain, weights, middle, sums),
        )
    )
    near[4] = (down, half, half), (up, 0, half)
    other[5] = (up, half, half), (right, 0, half)
    other[3] = (down, 0, half), (right, half, half)
    left, right = z_step(up[:, half:], 1), x_swap(up[:, :half])
    late = [(4, True, near[4])] + [(k, False, other[k]) for k in (5, 3)]
    sums = mix(place, gain, weights, late, sums)
    far = [(4, False, ((left, 0, half), (right, 0, half)))]
    return other_0, mix(place, gain, weights, far, sums, last=True)


INNER = 512
WIDE = INNER + 2 * STATE


def silu(values):
    return values / (1.0 + jnp.exp(-values))


def per_channel(values):
    head = lax.broadcasted_iota(jnp.int32, (128, INNER), 0)
    channel = lax.broadcasted_iota(jnp.int32, (128, INNER), 1)
    spread = (head == channel // SSM_HEAD_DIM).astype(BF16)
    return dot(values.astype(BF16), spread)


def conv_kernel(proj, tail, weight, bias, dt_bias, a_log, x_out, bc_out, cum_out, dt_out, msg, pad):
    pad[0:TAIL, :] = tail[...].astype(F32)
    pad[TAIL:, :] = proj[:, 0:WIDE].astype(F32)
    summed = bias[...] + weight[0:1, :] * pad[pl.ds(TAIL - CONV + 1, ROWS), :]
    for k in range(1, CONV):
        summed = summed + weight[k : k + 1, :] * pad[pl.ds(TAIL - CONV + 1 + k, ROWS), :]
    conv = silu(summed).astype(BF16)
    x_out[...] = conv[:, :INNER]
    bc_out[...] = conv[:, INNER:]
    raw = proj[:, WIDE:].astype(F32) + dt_bias[...]
    step = jnp.maximum(raw, 0.0) + jnp.log1p(jnp.exp(-jnp.abs(raw)))
    dt_out[...] = step
    rate = -jnp.exp(a_log[...]) * step
    later = lax.broadcasted_iota(jnp.int32, (BLOCK, BLOCK), 0)
    earlier = lax.broadcasted_iota(jnp.int32, (BLOCK, BLOCK), 1)
    lower = (later >= earlier).astype(F32)
    base = jnp.zeros((1, 128), F32)
    for k in range(ROWS // BLOCK):
        rows = slice(k * BLOCK, (k + 1) * BLOCK)
        here = dot(lower, rate[rows], precision=HIGHEST) + base
        cum_out[rows, :] = here
        base = here[BLOCK - 1 : BLOCK, :]
    left = step * jnp.exp(base - cum_out[...])
    weighted = (x_out[...].astype(F32) * per_channel(left)).astype(BF16)
    msg[0:STATE, :] = dot(bc_out[:, :STATE], weighted, ((0,), (0,))).astype(BF16)
    msg[STATE:, :] = per_channel(jnp.broadcast_to(jnp.exp(base), (16, 128))).astype(BF16)


def conv_and_state(proj, tail, weight, bias, dt_bias, a_log):
    return pl.pallas_call(
        conv_kernel,
        out_shape=(
            jax.ShapeDtypeStruct((ROWS, INNER), BF16),
            jax.ShapeDtypeStruct((ROWS, 2 * STATE), BF16),
            jax.ShapeDtypeStruct((ROWS, 128), F32),
            jax.ShapeDtypeStruct((ROWS, 128), F32),
            jax.ShapeDtypeStruct((MSG, INNER), BF16),
        ),
        in_specs=[whole()] * 6,
        out_specs=(whole(),) * 5,
        scratch_shapes=[pltpu.VMEM((ROWS + TAIL, WIDE), F32)],
        compiler_params=pltpu.CompilerParams(vmem_limit_bytes=32 * MIB),
        cost_estimate=pl.CostEstimate(
            flops=200_000_000, bytes_accessed=3_000_000, transcendentals=800_000
        ),
        name="conv_and_state",
    )(proj, tail, weight, bias, dt_bias, a_log)


def scan_kernel(x_ref, bc, cum, step, d_skip, out):
    lower = lax.broadcasted_iota(jnp.int32, (BLOCK, BLOCK), 0) >= lax.broadcasted_iota(
        jnp.int32, (BLOCK, BLOCK), 1
    )
    low_lane = lax.broadcasted_iota(jnp.int32, (BLOCK, 128), 1) < SSM_HEAD_DIM
    state = None
    for k in range(ROWS // BLOCK):
        rows = slice(k * BLOCK, (k + 1) * BLOCK)
        b, c = bc[rows, :STATE], bc[rows, STATE:]
        x = x_ref[rows, :]
        here = cum[rows, :]
        here_t, step_t = here.T, step[rows, :].T
        met = jnp.where(lower, dot(c, b, ((1,), (1,))), 0.0)
        parts = []
        for pair in range(4):
            left = []
            for h in (2 * pair, 2 * pair + 1):
                gap = jnp.minimum(here[:, h : h + 1] - here_t[h : h + 1, :], 0.0)
                left.append((met * jnp.exp(gap) * step_t[h : h + 1, :]).astype(BF16))
            xs = x[:, pair * 128 : (pair + 1) * 128]
            none = jnp.zeros_like(xs)
            right = jnp.concatenate([jnp.where(low_lane, xs, none), jnp.where(low_lane, none, xs)], 0)
            parts.append(dot(jnp.concatenate(left, axis=1), right))
        y = jnp.concatenate(parts, axis=1)
        last = here[BLOCK - 1 : BLOCK, :]
        if k:
            start = cum[k * BLOCK - 1 : k * BLOCK, :]
            y = y + dot(c, state.astype(BF16)) * per_channel(jnp.exp(here - start))
        out[rows, :] = y + d_skip[...] * x.astype(F32)
        if k < ROWS // BLOCK - 1:
            weighted = per_channel(step[rows, :] * jnp.exp(last - here)) * x.astype(F32)
            added = dot(b, weighted.astype(BF16), ((0,), (0,)))
            if k:
                kept = per_channel(jnp.broadcast_to(jnp.exp(last - start), (8, 128)))[0:1, :]
                state = state * kept + added
            else:
                state = added


def local_scan(x, bc, cum, step, d_skip):
    return pl.pallas_call(
        scan_kernel,
        out_shape=jax.ShapeDtypeStruct((ROWS, INNER), F32),
        in_specs=[whole()] * 5,
        out_specs=whole(),
        compiler_params=pltpu.CompilerParams(vmem_limit_bytes=32 * MIB),
        cost_estimate=pl.CostEstimate(
            flops=400_000_000, bytes_accessed=3_000_000, transcendentals=600_000
        ),
        name="local_scan",
    )(x, bc, cum, step, d_skip)


def gate_kernel(y, bc, cum, state, gate, out):
    carried = dot(bc[:, STATE:], state[...]) * per_channel(jnp.exp(cum[...]))
    out[...] = ((y[...] + carried) * silu(gate[...].astype(F32))).astype(BF16)


def finish(y, bc, cum, state, gate):
    return pl.pallas_call(
        gate_kernel,
        out_shape=jax.ShapeDtypeStruct((ROWS, INNER), BF16),
        in_specs=[whole()] * 5,
        out_specs=whole(),
        compiler_params=pltpu.CompilerParams(vmem_limit_bytes=32 * MIB),
        cost_estimate=pl.CostEstimate(
            flops=70_000_000, bytes_accessed=3_500_000, transcendentals=600_000
        ),
        name="gate",
    )(y, bc, cum, state, gate)


def then(earlier, later):
    return (earlier[0] * later[1] + later[0], earlier[1] * later[1])


def unpack(message):
    values = message.astype(F32)
    return values[:STATE], values[STATE : STATE + 1]


def packed(state, decay):
    rows = jnp.broadcast_to(decay, (16, decay.shape[1]))
    return jnp.concatenate([state, rows]).astype(BF16)


def meet(part, exchange, here):
    mine, theirs = unpack(part), unpack(exchange(part))
    first = tuple(jnp.where(here == 0, a, b) for a, b in zip(mine, theirs))
    second = tuple(jnp.where(here == 0, b, a) for a, b in zip(mine, theirs))
    before = (jnp.where(here == 0, 0.0, theirs[0]), jnp.where(here == 0, 1.0, theirs[1]))
    return before, then(first, second)


def earlier_state(message, ctx, beside):
    core, x_hi = jnp.bitwise_and(ctx, 1), jnp.bitwise_and(ctx // 2, 1)
    half = INNER // 2

    def mine(values):
        return lax.dynamic_slice_in_dim(values, core * half, half, 1)

    in_chip, chip = meet(message, lambda m: ctx_permute(m, lambda i: i ^ 1), core)
    chip = mine(packed(*chip))
    (theirs, beside) = lax.optimization_barrier((ctx_permute(chip, lambda i: i ^ 2), beside))
    in_pair, pair = meet(chip, lambda m: theirs, x_hi)
    pair = packed(*pair)
    near, mid, far = [
        unpack(lax.ppermute(pair, "ctx", [(i, i + 4 * d) for i in range(16 - 4 * d)]))
        for d in (1, 2, 3)
    ]
    incoming = then(then(then(far, mid), near), in_pair)[0].astype(BF16)
    across = ctx_permute(incoming, lambda i: i ^ 1)
    incoming = jnp.where(
        core == 0,
        jnp.concatenate([incoming, across], axis=1),
        jnp.concatenate([across, incoming], axis=1),
    )
    return (incoming.astype(F32) * in_chip[1] + in_chip[0]).astype(BF16), beside


def shards(
    query,
    key,
    value,
    out_weight,
    residual,
    norm_gain,
    w_zx,
    w_bc,
    w_dt,
    conv_x_weight,
    conv_x_bias,
    conv_bc_weight,
    conv_bc_bias,
    dt_bias,
    a_log,
    d_skip,
):
    tp, ctx = lax.axis_index("tp"), lax.axis_index("ctx")
    z, x_lo = tp // 2, jnp.bitwise_and(tp, 1)
    place = jnp.stack([ctx, x_lo * HALF, z, x_lo]).astype(jnp.int32)

    core = jnp.bitwise_and(ctx, 1)
    tie = lax.optimization_barrier
    mine = pack(place, key, value)
    mine, w_zx, w_bc, w_dt, query, w_send = tie((mine, w_zx, w_bc, w_dt, query, out_weight))
    across = ctx_permute(mine, lambda i: i ^ 2)
    below, above = y_step(mine, 1), y_step(mine, -1)
    q_other = x_swap(lax.dynamic_slice_in_dim(query, (1 - x_lo) * HALF, HALF, 0))
    mine_other = ctx_permute(mine, lambda i: i ^ 1)
    send_0 = lax.dynamic_slice_in_dim(w_send, core * 128, EARLY, 0)
    bc_here = lax.dynamic_slice_in_dim(w_bc, z * STATE, STATE, 2)
    w_dt = jnp.pad(w_dt, ((0, 0), (0, 120)))
    w_mix = jnp.concatenate([w_zx[:, 1], bc_here[:, 0], bc_here[:, 1], w_dt, w_zx[:, 0]], axis=1)
    across, below, above, q_other, mine_other, send_0, w_mix = tie(
        (across, below, above, q_other, mine_other, send_0, w_mix)
    )
    w_mix = lax.all_gather(w_mix, "ctx", axis=0, tiled=True)
    below_x, above_x = y_step(across, 1), y_step(across, -1)
    far = y_step(below[:ROWS], 1), y_step(above[ROWS:], -1)
    half_0 = x_swap(send_0)
    held = [mine, across, below, above, mine_other]
    held += [ctx_permute(part, lambda i: i ^ 1) for part in held[1:4]]
    q_own = lax.dynamic_slice_in_dim(query, x_lo * HALF, HALF, 0)
    state = attend(place, q_own, q_other, held)
    below_x, above_x, far, state, half_0, w_send = tie((below_x, above_x, far, state, half_0, w_send))
    far_x = y_step(below_x[:ROWS], 1), y_step(above_x[ROWS:], -1)
    half_1 = x_swap(lax.dynamic_slice_in_dim(w_send, core * 128 + EARLY, 128 - EARLY, 0))
    rest_0 = ctx_permute(half_0, lambda i: i ^ 1)
    late = [below_x, above_x, *far, *far_x]
    late += [ctx_permute(part, lambda i: i ^ 1) for part in late]
    state, late, half_1 = tie((state, late, half_1))
    rest_1 = ctx_permute(half_1, lambda i: i ^ 1)
    context = attend(place, q_own, q_other, late, state)
    parts = project(place, context, (out_weight, half_0, half_1, rest_0, rest_1))
    attended = sum_over_z(parts)
    residual_here = lax.dynamic_slice(residual, (x_lo * HALF, z * (D // Z)), (HALF, D // Z))
    piece = (residual_here.astype(F32) + attended).astype(BF16)
    other_piece, (proj, gate_in) = project_stream(place, norm_gain[None, :], w_mix, piece)
    stream_own = lax.dynamic_slice_in_dim(piece, x_lo * 256, 256, 1)
    stream_other = lax.dynamic_slice_in_dim(other_piece, x_lo * 256, 256, 1)
    stream = jnp.where(
        x_lo == 0,
        jnp.concatenate([stream_own, stream_other], axis=0),
        jnp.concatenate([stream_other, stream_own], axis=0),
    )
    tail = lax.ppermute(proj[ROWS - TAIL :, :WIDE], "ctx", [(i, i + 1) for i in range(15)])

    bc_weight = lax.dynamic_slice_in_dim(conv_bc_weight, z * STATE, STATE, 2)
    bc_bias = lax.dynamic_slice_in_dim(conv_bc_bias, z * STATE, STATE, 1)
    taps = jnp.concatenate([conv_x_weight, bc_weight.reshape(CONV, 2 * STATE)], axis=1)
    bias = jnp.concatenate([conv_x_bias, bc_bias.reshape(2 * STATE)])[None, :]
    lanes = ((0, 120),)
    x, bc, cum, step, message = conv_and_state(
        proj, tail, taps, bias, jnp.pad(dt_bias, lanes)[None, :], jnp.pad(a_log, lanes)[None, :]
    )
    skip = jnp.repeat(d_skip, SSM_HEAD_DIM)[None, :]
    state, y = earlier_state(message, ctx, local_scan(x, bc, cum, step, skip))
    return stream, finish(y, bc, cum, state, gate_in)


def solution(mesh):
    return jax.shard_map(
        shards,
        mesh=mesh,
        in_specs=(
            P("ctx", "tp"),
            P("ctx", None),
            P("ctx", None),
            P("tp", None),
            P("ctx", None),
            P(),
            P("ctx", None, "tp"),
            P("ctx", None, None),
            P("ctx", "tp"),
            P(None, "tp"),
            P("tp"),
            P(),
            P(),
            P("tp"),
            P("tp"),
            P("tp"),
        ),
        out_specs=(P("ctx", "tp"), P("ctx", "tp")),
        check_vma=False,
    )
```

```python
import functools
import math

import jax
import jax.numpy as jnp
from jax import lax
from jax.experimental import pallas as pl
from jax.experimental.pallas import tpu as pltpu
from jax.sharding import PartitionSpec as P

D = 4096
HEAD_DIM = 128
SSM_HEAD_DIM = 64
STATE = 128
CONV = 4
BLOCK = 128
NEG_BIG = -1e30
EPSILON = 1e-05
HIGHEST = lax.Precision.HIGHEST
F32 = jnp.float32
BF16 = jnp.bfloat16
MIB = 1024 * 1024

Y, Z = 4, 8
ROWS = 512
HALF = 256
EARLY = 48
TAIL = 16
MSG = STATE + 16


def ctx_permute(block, move):
    return lax.ppermute(block, "ctx", [(i, move(i)) for i in range(16)])


def tp_permute(block, move):
    return lax.ppermute(block, "tp", [(i, move(i)) for i in range(16)])


def y_step(block, d):
    return ctx_permute(block, lambda i: (i + 4 * d) % 16)


def z_step(block, d):
    return tp_permute(block, lambda i: (i + 2 * d) % 16)


def x_swap(block):
    return tp_permute(block, lambda i: i ^ 1)


def dot(a, b, dims=((1,), (0,)), precision=None):
    return lax.dot_general(a, b, (dims, ((), ())), precision=precision, preferred_element_type=F32)


def whole(memory=pltpu.VMEM):
    return pl.BlockSpec(memory_space=memory)


def pack_kernel(place, key, value, out):
    del place
    out[0:ROWS, :] = key[...]
    for j in range(4):
        rows = slice(j * HEAD_DIM, (j + 1) * HEAD_DIM)
        out[ROWS + j * HEAD_DIM : ROWS + (j + 1) * HEAD_DIM, :] = value[rows, :].T


def pack(place, key, value):
    column = pl.BlockSpec((ROWS, HEAD_DIM), lambda i, place: (0, place[2]))
    return pl.pallas_call(
        pack_kernel,
        out_shape=jax.ShapeDtypeStruct((2 * ROWS, HEAD_DIM), BF16),
        grid_spec=pltpu.PrefetchScalarGridSpec(
            num_scalar_prefetch=1,
            grid=(1,),
            in_specs=[column, column],
            out_specs=pl.BlockSpec((2 * ROWS, HEAD_DIM), lambda i, place: (0, 0)),
        ),
        name="pack",
    )(place, key, value)


FIRST = ((0, 0, 0, 0), (0, 1, 0, 1), (3, 0, 0, 2), (1, 0, 0, 3))
SECOND = ((3, 1, 0, 0), (1, 1, 0, 1), (2, 0, 1, 2), (2, 0, 2, 2), (2, 1, 1, 3), (2, 1, 2, 3))


def attend_kernel(homes, last, place, q_own, q_other, *refs):
    count = 2 * len(homes)
    pieces, refs = refs[:count], refs[count:]
    if last:
        (top_in, total_in, acc_in, out), (kv, top, total, acc) = refs[:4], refs[4:]
        top[...] = top_in[...]
        total[...] = total_in[...]
        acc[...] = acc_in[...]
    else:
        top, total, acc, kv = refs
        top[...] = jnp.full(top.shape, NEG_BIG, F32)
        total[...] = jnp.zeros(total.shape, F32)
        acc[...] = jnp.zeros(acc.shape, F32)
    me, x_lo = place[0], place[3]
    for i, piece in enumerate(pieces):
        _, _, part, at = homes[i % len(homes)]
        rows = slice((part - 1) * ROWS, part * ROWS) if part else slice(0, 2 * ROWS)
        kv[at + 4 * (i // len(homes)), rows, :] = piece[...]
    unit = math.log2(math.e) / math.sqrt(HEAD_DIM)

    def block(slot, masked):
        keys = kv[slot, 0:ROWS, :]
        values = jnp.concatenate(
            [kv[slot, ROWS + HEAD_DIM * j : ROWS + HEAD_DIM * (j + 1), :] for j in range(4)], axis=1
        )
        heads = range(4)
        scores = []
        for h in heads:
            source = q_own if h < 2 else q_other
            queries = source[:, (h % 2) * HEAD_DIM : (h % 2 + 1) * HEAD_DIM]
            scores.append(dot(keys, queries, ((1,), (1,))))
        if masked:
            key_at = lax.broadcasted_iota(jnp.int32, scores[0].shape, 0)
            row_at = lax.broadcasted_iota(jnp.int32, scores[0].shape, 1) + x_lo * HALF
            visible = key_at <= row_at
            scores = [jnp.where(visible, score, NEG_BIG) for score in scores]
        old = [top[h] for h in heads]
        new = [jnp.maximum(old[h], jnp.max(scores[h], axis=0, keepdims=True)) for h in heads]
        weights = [jnp.exp2((scores[h] - new[h]) * unit) for h in heads]
        factor = [jnp.exp2((old[h] - new[h]) * unit) for h in heads]
        sums = [jnp.sum(weights[h], axis=0, keepdims=True) for h in heads]
        mixed = [dot(values, weights[h].astype(BF16)) for h in heads]
        for h in heads:
            total[h] = total[h] * factor[h] + sums[h]
            acc[h] = acc[h] * factor[h] + mixed[h]
            top[h] = new[h]

    if not last:
        block(0, True)
    places = {at: (apart, crossed) for apart, crossed, _, at in homes}
    aparts = sum(places[at][0] << (2 * at) for at in range(4))
    crosses = sum(places[at][1] << (2 * at) for at in range(4))

    @pl.loop(0 if last else 1, 8)
    def _(slot):
        shift = 2 * jnp.bitwise_and(slot, 3)
        apart = jnp.bitwise_and(lax.shift_right_logical(jnp.int32(aparts), shift), 3)
        crossed = jnp.bitwise_and(lax.shift_right_logical(jnp.int32(crosses), shift), 3)
        y = jnp.bitwise_and(me // 4 + apart, 3)
        rest = jnp.bitwise_xor(jnp.bitwise_and(me, 3), crossed * 2 + slot // 4)

        @pl.when(y * 4 + rest < me)
        def _():
            block(slot, False)

    if last:
        for h in range(4):
            out[:, h * HEAD_DIM : (h + 1) * HEAD_DIM] = (acc[h] / total[h]).T.astype(BF16)


def attend(place, q_own, q_other, pieces, before=None):
    last = before is not None
    state = [
        jax.ShapeDtypeStruct((4, 1, HALF), F32),
        jax.ShapeDtypeStruct((4, 1, HALF), F32),
        jax.ShapeDtypeStruct((4, HEAD_DIM, HALF), F32),
    ]
    scratch = [pltpu.VMEM((8, 2 * ROWS, HEAD_DIM), BF16)]
    if last:
        scratch += [pltpu.VMEM(part.shape, part.dtype) for part in state]
    return pl.pallas_call(
        functools.partial(attend_kernel, SECOND if last else FIRST, last),
        out_shape=jax.ShapeDtypeStruct((HALF, 4 * HEAD_DIM), BF16) if last else state,
        in_specs=[whole(pltpu.SMEM), whole(), whole()]
        + [whole()] * (len(pieces) + (3 if last else 0)),
        out_specs=whole() if last else [whole()] * 3,
        scratch_shapes=scratch,
        compiler_params=pltpu.CompilerParams(vmem_limit_bytes=32 * MIB),
        cost_estimate=pl.CostEstimate(
            flops=1_000_000, bytes_accessed=1_000_000, transcendentals=0
        ),
        name="attend_rest" if last else "attend_first",
    )(place, q_own, q_other, *pieces, *(before or ()))


def project_kernel(place, context, w_own, half_0, half_1, rest_0, rest_1, *refs):
    parts, weight = refs[:9], refs[9]
    core, z = jnp.bitwise_and(place[0], 1), place[2]
    weight[0:HALF, :] = w_own[...]
    for first, second, which in ((half_0, half_1, core), (rest_0, rest_1, 1 - core)):
        start = pl.multiple_of(HALF + which * 128, 128)
        weight[pl.ds(start, EARLY), :] = first[...]
        weight[pl.ds(start + EARLY, 128 - EARLY), :] = second[...]
    wide = D // Z
    for k in range(Z):
        column = pl.multiple_of(jnp.bitwise_and(z + k, Z - 1) * wide, wide)
        part = dot(context[...], weight[:, pl.ds(column, wide)]).astype(BF16)
        if k == 4:
            parts[4][...] = part[:, : wide // 2]
            parts[8][...] = part[:, wide // 2 :]
        else:
            parts[k][...] = part


def project(place, context, weights):
    wide = D // Z
    out = [jax.ShapeDtypeStruct((HALF, wide // 2 if k in (4, 8) else wide), BF16) for k in range(9)]
    return pl.pallas_call(
        project_kernel,
        out_shape=out,
        in_specs=[whole(pltpu.SMEM)] + [whole()] * 6,
        out_specs=[whole()] * 9,
        scratch_shapes=[pltpu.VMEM((ROWS, D), BF16)],
        compiler_params=pltpu.CompilerParams(vmem_limit_bytes=32 * MIB),
        cost_estimate=pl.CostEstimate(
            flops=1_100_000_000, bytes_accessed=6_500_000, transcendentals=0
        ),
        name="project",
    )(place, context, *weights)


def sum_over_z(parts):
    half = parts[4].shape[1]
    up, down = z_step(parts[4], 1), z_step(parts[8], -1)
    third, fifth = parts[3].astype(F32), parts[5].astype(F32)
    up = jnp.concatenate([third[:, :half] + up.astype(F32), third[:, half:]], axis=1)
    down = jnp.concatenate([fifth[:, :half], fifth[:, half:] + down.astype(F32)], axis=1)
    for k in (2, 1, 0):
        up, down = lax.optimization_barrier((up.astype(BF16), down.astype(BF16)))
        up, down = z_step(up, 1), z_step(down, -1)
        if k:
            up = parts[k].astype(F32) + up.astype(F32)
            down = parts[8 - k].astype(F32) + down.astype(F32)
    return parts[0].astype(F32) + up.astype(F32) + down.astype(F32)


MIXED = 1408


def mix_kernel(steps, first, last, place, gain, weights, *refs):
    count = 1 + max(array for _, _, sources in steps for array, _, _ in sources)
    blocks, refs = refs[:count], refs[count:]
    if not first:
        (square_in, acc_in), refs = refs[:2], refs[2:]
    (square, acc), (held, sems) = refs[:2], refs[2:4]
    if last:
        total, squares = refs[4], refs[5]
    else:
        total, squares = acc, square
    z, x_lo = place[2], place[3]
    wide = D // Z
    apart = []
    for k, _, _ in steps:
        if k not in apart:
            apart.append(k)
    starts = [pl.multiple_of(jnp.bitwise_and(z + k, Z - 1) * wide, wide) for k in apart]
    copies = [
        pltpu.make_async_copy(weights.at[pl.ds(start, wide)], held.at[i], sems.at[i])
        for i, start in enumerate(starts)
    ]
    for copy in copies:
        copy.start()
    if first:
        squares[...] = jnp.zeros(squares.shape, F32)
        total[...] = jnp.zeros(total.shape, F32)
    else:
        squares[...] = square_in[...]
        total[...] = acc_in[...]
    waited = set()
    for k, own, sources in steps:
        i = apart.index(k)
        if k not in waited:
            waited.add(k)
            copies[i].wait()
        rows = pl.ds(pl.multiple_of((x_lo if own else 1 - x_lo) * HALF, HALF), HALF)
        parts = [blocks[array][:, at : at + width] for array, at, width in sources]
        value = (jnp.concatenate(parts, axis=1) if len(parts) > 1 else parts[0]).astype(F32)
        square_sum = value * value
        squares[rows, :] += sum(square_sum[:, j * 128 : (j + 1) * 128] for j in range(wide // 128))
        scaled = (value * gain[:, pl.ds(starts[i], wide)]).astype(BF16)
        total[rows, :] += dot(scaled, held[i])
    if last:
        proj, gate = square, acc
        mean = jnp.sum(squares[...], axis=1, keepdims=True) * (1.0 / D)
        result = (total[...] * lax.rsqrt(mean + EPSILON)).astype(BF16)
        proj[...] = result[:, INNER:]
        gate[...] = result[:, :INNER]


def mix(place, gain, weights, steps, before=None, last=False):
    blocks, plan = [], []
    for k, own, sources in steps:
        found = []
        for array, at, width in sources:
            known = [i for i, block in enumerate(blocks) if block is array]
            if not known:
                known = [len(blocks)]
                blocks.append(array)
            found.append((known[0], at, width))
        plan.append((k, own, tuple(found)))
    apart = len({k for k, _, _ in steps})
    sums = [(ROWS, 128), (ROWS, MIXED)]
    if last:
        out = [
            jax.ShapeDtypeStruct((ROWS, MIXED - INNER), BF16),
            jax.ShapeDtypeStruct((ROWS, INNER), BF16),
        ]
    else:
        out = [jax.ShapeDtypeStruct(shape, F32) for shape in sums]
    scratch = [
        pltpu.VMEM((apart, D // Z, MIXED), BF16),
        pltpu.SemaphoreType.DMA((apart,)),
    ]
    if last:
        scratch += [pltpu.VMEM(sums[1], F32), pltpu.VMEM(sums[0], F32)]
    flops = 2 * HALF * (D // Z) * MIXED * len(steps)
    return pl.pallas_call(
        functools.partial(mix_kernel, tuple(plan), before is None, last),
        out_shape=out,
        in_specs=[whole(pltpu.SMEM), whole(), whole(pl.ANY)]
        + [whole()] * (len(blocks) + (0 if before is None else 2)),
        out_specs=[whole()] * 2,
        scratch_shapes=scratch,
        compiler_params=pltpu.CompilerParams(vmem_limit_bytes=40 * MIB),
        cost_estimate=pl.CostEstimate(
            flops=flops, bytes_accessed=1_500_000 * apart + 6_000_000, transcendentals=0
        ),
        name="mix_last" if last else "mix",
    )(place, gain, weights, *blocks, *(before or ()))


def project_stream(place, gain, weights, piece):
    wide = piece.shape[1]
    half = wide // 2
    tie = lax.optimization_barrier

    def joined(*blocks):
        return jnp.concatenate(blocks, axis=1)

    up, down, other_0 = tie((z_step(piece, 1), z_step(piece, -1), x_swap(piece)))
    left = other_0[:, :half]
    near_up, near_down = (up, 0), (down, 0)
    up, down = joined(up, left), joined(left, down)
    near = {0: ((piece, 0, wide),), 7: ((*near_up, wide),), 1: ((*near_down, wide),)}
    other = {0: ((other_0, 0, wide),)}
    sums = None
    for k in (1, 2):
        right = joined(up[:, half:wide], down[:, wide:])
        got = (z_step(up, 1), z_step(down, -1), x_swap(right))
        if k == 2:
            early = [(0, True, near[0]), (0, False, other[0])]
            early += [(j, own, from_[j]) for j in (7, 1) for own, from_ in ((True, near), (False, other))]
            early += [(j, True, near[j]) for j in (6, 2)]
            got = tie((*got, *mix(place, gain, weights, early)))
            got, sums = got[:3], got[3:]
        else:
            got = tie(got)
        up, down, right = got
        near[7 - k], near[k + 1] = ((up, 0, wide),), ((down, half, wide),)
        other[8 - k] = (up, wide, half), (right, 0, half)
        other[k] = (down, 0, half), (right, half, half)
    middle = [(k, True, near[k]) for k in (5, 3)] + [(k, False, other[k]) for k in (6, 2)]
    right = joined(up[:, half:wide], down[:, wide:])
    up, down, right, sums = tie(
        (
            z_step(up[:, half:], 1),
            z_step(down[:, :wide], -1),
            x_swap(right),
            mix(place, gain, weights, middle, sums),
        )
    )
    near[4] = (down, half, half), (up, 0, half)
    other[5] = (up, half, half), (right, 0, half)
    other[3] = (down, 0, half), (right, half, half)
    left, right = z_step(up[:, half:], 1), x_swap(up[:, :half])
    late = [(4, True, near[4])] + [(k, False, other[k]) for k in (5, 3)]
    sums = mix(place, gain, weights, late, sums)
    far = [(4, False, ((left, 0, half), (right, 0, half)))]
    return other_0, mix(place, gain, weights, far, sums, last=True)


INNER = 512
WIDE = INNER + 2 * STATE


def silu(values):
    return values / (1.0 + jnp.exp(-values))


def per_channel(values):
    head = lax.broadcasted_iota(jnp.int32, (128, INNER), 0)
    channel = lax.broadcasted_iota(jnp.int32, (128, INNER), 1)
    spread = (head == channel // SSM_HEAD_DIM).astype(BF16)
    return dot(values.astype(BF16), spread)


def conv_kernel(proj, tail, weight, bias, dt_bias, a_log, x_out, bc_out, cum_out, dt_out, msg, pad):
    pad[0:TAIL, :] = tail[...].astype(F32)
    pad[TAIL:, :] = proj[:, 0:WIDE].astype(F32)
    summed = bias[...] + weight[0:1, :] * pad[pl.ds(TAIL - CONV + 1, ROWS), :]
    for k in range(1, CONV):
        summed = summed + weight[k : k + 1, :] * pad[pl.ds(TAIL - CONV + 1 + k, ROWS), :]
    conv = silu(summed).astype(BF16)
    x_out[...] = conv[:, :INNER]
    bc_out[...] = conv[:, INNER:]
    raw = proj[:, WIDE:].astype(F32) + dt_bias[...]
    step = jnp.maximum(raw, 0.0) + jnp.log1p(jnp.exp(-jnp.abs(raw)))
    dt_out[...] = step
    rate = -jnp.exp(a_log[...]) * step
    later = lax.broadcasted_iota(jnp.int32, (BLOCK, BLOCK), 0)
    earlier = lax.broadcasted_iota(jnp.int32, (BLOCK, BLOCK), 1)
    lower = (later >= earlier).astype(F32)
    base = jnp.zeros((1, 128), F32)
    for k in range(ROWS // BLOCK):
        rows = slice(k * BLOCK, (k + 1) * BLOCK)
        here = dot(lower, rate[rows], precision=HIGHEST) + base
        cum_out[rows, :] = here
        base = here[BLOCK - 1 : BLOCK, :]
    left = step * jnp.exp(base - cum_out[...])
    weighted = (x_out[...].astype(F32) * per_channel(left)).astype(BF16)
    msg[0:STATE, :] = dot(bc_out[:, :STATE], weighted, ((0,), (0,))).astype(BF16)
    msg[STATE:, :] = per_channel(jnp.broadcast_to(jnp.exp(base), (16, 128))).astype(BF16)


def conv_and_state(proj, tail, weight, bias, dt_bias, a_log):
    return pl.pallas_call(
        conv_kernel,
        out_shape=(
            jax.ShapeDtypeStruct((ROWS, INNER), BF16),
            jax.ShapeDtypeStruct((ROWS, 2 * STATE), BF16),
            jax.ShapeDtypeStruct((ROWS, 128), F32),
            jax.ShapeDtypeStruct((ROWS, 128), F32),
            jax.ShapeDtypeStruct((MSG, INNER), BF16),
        ),
        in_specs=[whole()] * 6,
        out_specs=(whole(),) * 5,
        scratch_shapes=[pltpu.VMEM((ROWS + TAIL, WIDE), F32)],
        compiler_params=pltpu.CompilerParams(vmem_limit_bytes=32 * MIB),
        cost_estimate=pl.CostEstimate(
            flops=200_000_000, bytes_accessed=3_000_000, transcendentals=800_000
        ),
        name="conv_and_state",
    )(proj, tail, weight, bias, dt_bias, a_log)


def scan_kernel(x_ref, bc, cum, step, d_skip, out):
    lower = lax.broadcasted_iota(jnp.int32, (BLOCK, BLOCK), 0) >= lax.broadcasted_iota(
        jnp.int32, (BLOCK, BLOCK), 1
    )
    low_lane = lax.broadcasted_iota(jnp.int32, (BLOCK, 128), 1) < SSM_HEAD_DIM
    state = None
    for k in range(ROWS // BLOCK):
        rows = slice(k * BLOCK, (k + 1) * BLOCK)
        b, c = bc[rows, :STATE], bc[rows, STATE:]
        x = x_ref[rows, :]
        here = cum[rows, :]
        here_t, step_t = here.T, step[rows, :].T
        met = jnp.where(lower, dot(c, b, ((1,), (1,))), 0.0)
        parts = []
        for pair in range(4):
            left = []
            for h in (2 * pair, 2 * pair + 1):
                gap = jnp.minimum(here[:, h : h + 1] - here_t[h : h + 1, :], 0.0)
                left.append((met * jnp.exp(gap) * step_t[h : h + 1, :]).astype(BF16))
            xs = x[:, pair * 128 : (pair + 1) * 128]
            none = jnp.zeros_like(xs)
            right = jnp.concatenate([jnp.where(low_lane, xs, none), jnp.where(low_lane, none, xs)], 0)
            parts.append(dot(jnp.concatenate(left, axis=1), right))
        y = jnp.concatenate(parts, axis=1)
        last = here[BLOCK - 1 : BLOCK, :]
        if k:
            start = cum[k * BLOCK - 1 : k * BLOCK, :]
            y = y + dot(c, state.astype(BF16)) * per_channel(jnp.exp(here - start))
        out[rows, :] = y + d_skip[...] * x.astype(F32)
        if k < ROWS // BLOCK - 1:
            weighted = per_channel(step[rows, :] * jnp.exp(last - here)) * x.astype(F32)
            added = dot(b, weighted.astype(BF16), ((0,), (0,)))
            if k:
                kept = per_channel(jnp.broadcast_to(jnp.exp(last - start), (8, 128)))[0:1, :]
                state = state * kept + added
            else:
                state = added


def local_scan(x, bc, cum, step, d_skip):
    return pl.pallas_call(
        scan_kernel,
        out_shape=jax.ShapeDtypeStruct((ROWS, INNER), F32),
        in_specs=[whole()] * 5,
        out_specs=whole(),
        compiler_params=pltpu.CompilerParams(vmem_limit_bytes=32 * MIB),
        cost_estimate=pl.CostEstimate(
            flops=400_000_000, bytes_accessed=3_000_000, transcendentals=600_000
        ),
        name="local_scan",
    )(x, bc, cum, step, d_skip)


def gate_kernel(y, bc, cum, state, gate, out):
    carried = dot(bc[:, STATE:], state[...]) * per_channel(jnp.exp(cum[...]))
    out[...] = ((y[...] + carried) * silu(gate[...].astype(F32))).astype(BF16)


def finish(y, bc, cum, state, gate):
    return pl.pallas_call(
        gate_kernel,
        out_shape=jax.ShapeDtypeStruct((ROWS, INNER), BF16),
        in_specs=[whole()] * 5,
        out_specs=whole(),
        compiler_params=pltpu.CompilerParams(vmem_limit_bytes=32 * MIB),
        cost_estimate=pl.CostEstimate(
            flops=70_000_000, bytes_accessed=3_500_000, transcendentals=600_000
        ),
        name="gate",
    )(y, bc, cum, state, gate)


def then(earlier, later):
    return (earlier[0] * later[1] + later[0], earlier[1] * later[1])


def unpack(message):
    values = message.astype(F32)
    return values[:STATE], values[STATE : STATE + 1]


def packed(state, decay):
    rows = jnp.broadcast_to(decay, (16, decay.shape[1]))
    return jnp.concatenate([state, rows]).astype(BF16)


def meet(part, exchange, here):
    mine, theirs = unpack(part), unpack(exchange(part))
    first = tuple(jnp.where(here == 0, a, b) for a, b in zip(mine, theirs))
    second = tuple(jnp.where(here == 0, b, a) for a, b in zip(mine, theirs))
    before = (jnp.where(here == 0, 0.0, theirs[0]), jnp.where(here == 0, 1.0, theirs[1]))
    return before, then(first, second)


def earlier_state(message, ctx, beside):
    core, x_hi = jnp.bitwise_and(ctx, 1), jnp.bitwise_and(ctx // 2, 1)
    half = INNER // 2

    def mine(values):
        return lax.dynamic_slice_in_dim(values, core * half, half, 1)

    in_chip, chip = meet(message, lambda m: ctx_permute(m, lambda i: i ^ 1), core)
    chip = mine(packed(*chip))
    (theirs, beside) = lax.optimization_barrier((ctx_permute(chip, lambda i: i ^ 2), beside))
    in_pair, pair = meet(chip, lambda m: theirs, x_hi)
    pair = packed(*pair)
    near, mid, far = [
        unpack(lax.ppermute(pair, "ctx", [(i, i + 4 * d) for i in range(16 - 4 * d)]))
        for d in (1, 2, 3)
    ]
    incoming = then(then(then(far, mid), near), in_pair)[0].astype(BF16)
    across = ctx_permute(incoming, lambda i: i ^ 1)
    incoming = jnp.where(
        core == 0,
        jnp.concatenate([incoming, across], axis=1),
        jnp.concatenate([across, incoming], axis=1),
    )
    return (incoming.astype(F32) * in_chip[1] + in_chip[0]).astype(BF16), beside


def shards(
    query,
    key,
    value,
    out_weight,
    residual,
    norm_gain,
    w_zx,
    w_bc,
    w_dt,
    conv_x_weight,
    conv_x_bias,
    conv_bc_weight,
    conv_bc_bias,
    dt_bias,
    a_log,
    d_skip,
):
    tp, ctx = lax.axis_index("tp"), lax.axis_index("ctx")
    z, x_lo = tp // 2, jnp.bitwise_and(tp, 1)
    place = jnp.stack([ctx, x_lo * HALF, z, x_lo]).astype(jnp.int32)

    core = jnp.bitwise_and(ctx, 1)
    tie = lax.optimization_barrier
    mine = pack(place, key, value)
    mine, w_zx, w_bc, w_dt, query, w_send = tie((mine, w_zx, w_bc, w_dt, query, out_weight))
    across = ctx_permute(mine, lambda i: i ^ 2)
    below, above = y_step(mine, 1), y_step(mine, -1)
    q_other = x_swap(lax.dynamic_slice_in_dim(query, (1 - x_lo) * HALF, HALF, 0))
    mine_other = ctx_permute(mine, lambda i: i ^ 1)
    half_0 = x_swap(lax.dynamic_slice_in_dim(w_send, core * 128, EARLY, 0))
    w_send = lax.dynamic_slice_in_dim(w_send, core * 128 + EARLY, 128 - EARLY, 0)
    bc_here = lax.dynamic_slice_in_dim(w_bc, z * STATE, STATE, 2)
    w_dt = jnp.pad(w_dt, ((0, 0), (0, 120)))
    w_zx = w_zx.reshape(w_zx.shape[0], 2 * INNER)
    w_mix = jnp.concatenate([w_zx, bc_here[:, 0], bc_here[:, 1], w_dt], axis=1)
    across, below, above, q_other, mine_other, half_0, w_send, w_mix = tie(
        (across, below, above, q_other, mine_other, half_0, w_send, w_mix)
    )
    w_mix = lax.all_gather(w_mix, "ctx", axis=0, tiled=True)
    below_x, above_x = y_step(across, 1), y_step(across, -1)
    far = y_step(below[:ROWS], 1), y_step(above[ROWS:], -1)
    half_1 = x_swap(w_send)
    held = [mine, across, below, above, mine_other]
    held += [ctx_permute(part, lambda i: i ^ 1) for part in held[1:4]]
    q_own = lax.dynamic_slice_in_dim(query, x_lo * HALF, HALF, 0)
    state = attend(place, q_own, q_other, held)
    below_x, above_x, far, state, half_1 = tie((below_x, above_x, far, state, half_1))
    far_x = y_step(below_x[:ROWS], 1), y_step(above_x[ROWS:], -1)
    rest_0, rest_1 = [ctx_permute(half, lambda i: i ^ 1) for half in (half_0, half_1)]
    late = [below_x, above_x, *far, *far_x]
    late += [ctx_permute(part, lambda i: i ^ 1) for part in late]
    state, late = tie((state, late))
    context = attend(place, q_own, q_other, late, state)
    parts = project(place, context, (out_weight, half_0, half_1, rest_0, rest_1))
    attended = sum_over_z(parts)
    residual_here = lax.dynamic_slice(residual, (x_lo * HALF, z * (D // Z)), (HALF, D // Z))
    piece = (residual_here.astype(F32) + attended).astype(BF16)
    other_piece, (proj, gate_in) = project_stream(place, norm_gain[None, :], w_mix, piece)
    stream_own = lax.dynamic_slice_in_dim(piece, x_lo * 256, 256, 1)
    stream_other = lax.dynamic_slice_in_dim(other_piece, x_lo * 256, 256, 1)
    stream = jnp.where(
        x_lo == 0,
        jnp.concatenate([stream_own, stream_other], axis=0),
        jnp.concatenate([stream_other, stream_own], axis=0),
    )
    tail = lax.ppermute(proj[ROWS - TAIL :, :WIDE], "ctx", [(i, i + 1) for i in range(15)])

    bc_weight = lax.dynamic_slice_in_dim(conv_bc_weight, z * STATE, STATE, 2)
    bc_bias = lax.dynamic_slice_in_dim(conv_bc_bias, z * STATE, STATE, 1)
    taps = jnp.concatenate([conv_x_weight, bc_weight.reshape(CONV, 2 * STATE)], axis=1)
    bias = jnp.concatenate([conv_x_bias, bc_bias.reshape(2 * STATE)])[None, :]
    lanes = ((0, 120),)
    x, bc, cum, step, message = conv_and_state(
        proj, tail, taps, bias, jnp.pad(dt_bias, lanes)[None, :], jnp.pad(a_log, lanes)[None, :]
    )
    skip = jnp.repeat(d_skip, SSM_HEAD_DIM)[None, :]
    state, y = earlier_state(message, ctx, local_scan(x, bc, cum, step, skip))
    return stream, finish(y, bc, cum, state, gate_in)


def solution(mesh):
    return jax.shard_map(
        shards,
        mesh=mesh,
        in_specs=(
            P("ctx", "tp"),
            P("ctx", None),
            P("ctx", None),
            P("tp", None),
            P("ctx", None),
            P(),
            P("ctx", None, "tp"),
            P("ctx", None, None),
            P("ctx", "tp"),
            P(None, "tp"),
            P("tp"),
            P(),
            P(),
            P("tp"),
            P("tp"),
            P("tp"),
        ),
        out_specs=(P("ctx", "tp"), P("ctx", "tp")),
        check_vma=False,
    )
```

```python
import functools
import math

import jax
import jax.numpy as jnp
from jax import lax
from jax.experimental import pallas as pl
from jax.experimental.pallas import tpu as pltpu
from jax.sharding import PartitionSpec as P

D = 4096
HEAD_DIM = 128
SSM_HEAD_DIM = 64
STATE = 128
CONV = 4
BLOCK = 128
NEG_BIG = -1e30
EPSILON = 1e-05
HIGHEST = lax.Precision.HIGHEST
F32 = jnp.float32
BF16 = jnp.bfloat16
MIB = 1024 * 1024

Y, Z = 4, 8
ROWS = 512
HALF = 256
EARLY = 48
TAIL = 16
MSG = STATE + 16


def ctx_permute(block, move):
    return lax.ppermute(block, "ctx", [(i, move(i)) for i in range(16)])


def tp_permute(block, move):
    return lax.ppermute(block, "tp", [(i, move(i)) for i in range(16)])


def y_step(block, d):
    return ctx_permute(block, lambda i: (i + 4 * d) % 16)


def z_step(block, d):
    return tp_permute(block, lambda i: (i + 2 * d) % 16)


def x_swap(block):
    return tp_permute(block, lambda i: i ^ 1)


def dot(a, b, dims=((1,), (0,)), precision=None):
    return lax.dot_general(a, b, (dims, ((), ())), precision=precision, preferred_element_type=F32)


def whole(memory=pltpu.VMEM):
    return pl.BlockSpec(memory_space=memory)


def pack_kernel(place, key, value, out):
    del place
    out[0:ROWS, :] = key[...]
    for j in range(4):
        rows = slice(j * HEAD_DIM, (j + 1) * HEAD_DIM)
        out[ROWS + j * HEAD_DIM : ROWS + (j + 1) * HEAD_DIM, :] = value[rows, :].T


def pack(place, key, value):
    column = pl.BlockSpec((ROWS, HEAD_DIM), lambda i, place: (0, place[2]))
    return pl.pallas_call(
        pack_kernel,
        out_shape=jax.ShapeDtypeStruct((2 * ROWS, HEAD_DIM), BF16),
        grid_spec=pltpu.PrefetchScalarGridSpec(
            num_scalar_prefetch=1,
            grid=(1,),
            in_specs=[column, column],
            out_specs=pl.BlockSpec((2 * ROWS, HEAD_DIM), lambda i, place: (0, 0)),
        ),
        name="pack",
    )(place, key, value)


FIRST = ((0, 0), (0, 1), (3, 0), (1, 0), (2, 0))
SECOND = ((3, 1), (1, 1), (2, 1))


def attend_kernel(homes, last, place, q_own, q_other, *refs):
    count = 2 * len(homes)
    pieces, refs = refs[:count], refs[count:]
    if last:
        (top_in, total_in, acc_in, out), (kv, top, total, acc) = refs[:4], refs[4:]
        top[...] = top_in[...]
        total[...] = total_in[...]
        acc[...] = acc_in[...]
    else:
        top, total, acc, kv = refs
        top[...] = jnp.full(top.shape, NEG_BIG, F32)
        total[...] = jnp.zeros(total.shape, F32)
        acc[...] = jnp.zeros(acc.shape, F32)
    me, x_lo = place[0], place[3]
    for slot, piece in enumerate(pieces):
        kv[slot] = piece[...]
    unit = math.log2(math.e) / math.sqrt(HEAD_DIM)

    def block(slot, masked):
        keys = kv[slot, 0:ROWS, :]
        values = jnp.concatenate(
            [kv[slot, ROWS + HEAD_DIM * j : ROWS + HEAD_DIM * (j + 1), :] for j in range(4)], axis=1
        )
        heads = range(4)
        scores = []
        for h in heads:
            source = q_own if h < 2 else q_other
            queries = source[:, (h % 2) * HEAD_DIM : (h % 2 + 1) * HEAD_DIM]
            scores.append(dot(keys, queries, ((1,), (1,))))
        if masked:
            key_at = lax.broadcasted_iota(jnp.int32, scores[0].shape, 0)
            row_at = lax.broadcasted_iota(jnp.int32, scores[0].shape, 1) + x_lo * HALF
            visible = key_at <= row_at
            scores = [jnp.where(visible, score, NEG_BIG) for score in scores]
        old = [top[h] for h in heads]
        new = [jnp.maximum(old[h], jnp.max(scores[h], axis=0, keepdims=True)) for h in heads]
        weights = [jnp.exp2((scores[h] - new[h]) * unit) for h in heads]
        factor = [jnp.exp2((old[h] - new[h]) * unit) for h in heads]
        sums = [jnp.sum(weights[h], axis=0, keepdims=True) for h in heads]
        mixed = [dot(values, weights[h].astype(BF16)) for h in heads]
        for h in heads:
            total[h] = total[h] * factor[h] + sums[h]
            acc[h] = acc[h] * factor[h] + mixed[h]
            top[h] = new[h]

    if not last:
        block(0, True)
    each = len(homes)
    aparts = sum(apart << (2 * i) for i, (apart, _) in enumerate(homes))
    crosses = sum(crossed << (2 * i) for i, (_, crossed) in enumerate(homes))

    @pl.loop(0 if last else 1, 2 * each)
    def _(slot):
        other = (slot >= each).astype(jnp.int32)
        shift = 2 * (slot - other * each)
        apart = jnp.bitwise_and(lax.shift_right_logical(jnp.int32(aparts), shift), 3)
        crossed = jnp.bitwise_and(lax.shift_right_logical(jnp.int32(crosses), shift), 3)
        y = jnp.bitwise_and(me // 4 + apart, 3)
        rest = jnp.bitwise_xor(jnp.bitwise_and(me, 3), crossed * 2 + other)

        @pl.when(y * 4 + rest < me)
        def _():
            block(slot, False)

    if last:
        for h in range(4):
            out[:, h * HEAD_DIM : (h + 1) * HEAD_DIM] = (acc[h] / total[h]).T.astype(BF16)


def attend(place, q_own, q_other, pieces, before=None):
    last = before is not None
    state = [
        jax.ShapeDtypeStruct((4, 1, HALF), F32),
        jax.ShapeDtypeStruct((4, 1, HALF), F32),
        jax.ShapeDtypeStruct((4, HEAD_DIM, HALF), F32),
    ]
    scratch = [pltpu.VMEM((len(pieces), 2 * ROWS, HEAD_DIM), BF16)]
    if last:
        scratch += [pltpu.VMEM(part.shape, part.dtype) for part in state]
    return pl.pallas_call(
        functools.partial(attend_kernel, SECOND if last else FIRST, last),
        out_shape=jax.ShapeDtypeStruct((HALF, 4 * HEAD_DIM), BF16) if last else state,
        in_specs=[whole(pltpu.SMEM), whole(), whole()]
        + [whole()] * (len(pieces) + (3 if last else 0)),
        out_specs=whole() if last else [whole()] * 3,
        scratch_shapes=scratch,
        compiler_params=pltpu.CompilerParams(vmem_limit_bytes=32 * MIB),
        cost_estimate=pl.CostEstimate(
            flops=1_000_000, bytes_accessed=1_000_000, transcendentals=0
        ),
        name="attend_rest" if last else "attend_first",
    )(place, q_own, q_other, *pieces, *(before or ()))


def project_kernel(place, context, w_own, half_0, half_1, rest_0, rest_1, *refs):
    parts, weight = refs[:9], refs[9]
    core, z = jnp.bitwise_and(place[0], 1), place[2]
    weight[0:HALF, :] = w_own[...]
    for first, second, which in ((half_0, half_1, core), (rest_0, rest_1, 1 - core)):
        start = pl.multiple_of(HALF + which * 128, 128)
        weight[pl.ds(start, EARLY), :] = first[...]
        weight[pl.ds(start + EARLY, 128 - EARLY), :] = second[...]
    wide = D // Z
    for k in range(Z):
        column = pl.multiple_of(jnp.bitwise_and(z + k, Z - 1) * wide, wide)
        part = dot(context[...], weight[:, pl.ds(column, wide)]).astype(BF16)
        if k == 4:
            parts[4][...] = part[:, : wide // 2]
            parts[8][...] = part[:, wide // 2 :]
        else:
            parts[k][...] = part


def project(place, context, weights):
    wide = D // Z
    out = [jax.ShapeDtypeStruct((HALF, wide // 2 if k in (4, 8) else wide), BF16) for k in range(9)]
    return pl.pallas_call(
        project_kernel,
        out_shape=out,
        in_specs=[whole(pltpu.SMEM)] + [whole()] * 6,
        out_specs=[whole()] * 9,
        scratch_shapes=[pltpu.VMEM((ROWS, D), BF16)],
        compiler_params=pltpu.CompilerParams(vmem_limit_bytes=32 * MIB),
        cost_estimate=pl.CostEstimate(
            flops=1_100_000_000, bytes_accessed=6_500_000, transcendentals=0
        ),
        name="project",
    )(place, context, *weights)


def sum_over_z(parts):
    half = parts[4].shape[1]
    up, down = z_step(parts[4], 1), z_step(parts[8], -1)
    third, fifth = parts[3].astype(F32), parts[5].astype(F32)
    up = jnp.concatenate([third[:, :half] + up.astype(F32), third[:, half:]], axis=1)
    down = jnp.concatenate([fifth[:, :half], fifth[:, half:] + down.astype(F32)], axis=1)
    for k in (2, 1, 0):
        up, down = lax.optimization_barrier((up.astype(BF16), down.astype(BF16)))
        up, down = z_step(up, 1), z_step(down, -1)
        if k:
            up = parts[k].astype(F32) + up.astype(F32)
            down = parts[8 - k].astype(F32) + down.astype(F32)
    return parts[0].astype(F32) + up.astype(F32) + down.astype(F32)


MIXED = 1408


def mix_kernel(steps, first, last, place, gain, weights, *refs):
    count = 1 + max(array for _, _, sources in steps for array, _, _ in sources)
    blocks, refs = refs[:count], refs[count:]
    if not first:
        (square_in, acc_in), refs = refs[:2], refs[2:]
    (square, acc), (held, sems) = refs[:2], refs[2:4]
    if last:
        total, squares = refs[4], refs[5]
    else:
        total, squares = acc, square
    z, x_lo = place[2], place[3]
    wide = D // Z
    apart = []
    for k, _, _ in steps:
        if k not in apart:
            apart.append(k)
    starts = [pl.multiple_of(jnp.bitwise_and(z + k, Z - 1) * wide, wide) for k in apart]
    copies = [
        pltpu.make_async_copy(weights.at[pl.ds(start, wide)], held.at[i], sems.at[i])
        for i, start in enumerate(starts)
    ]
    for copy in copies:
        copy.start()
    if first:
        squares[...] = jnp.zeros(squares.shape, F32)
        total[...] = jnp.zeros(total.shape, F32)
    else:
        squares[...] = square_in[...]
        total[...] = acc_in[...]
    waited = set()
    for k, own, sources in steps:
        i = apart.index(k)
        if k not in waited:
            waited.add(k)
            copies[i].wait()
        rows = pl.ds(pl.multiple_of((x_lo if own else 1 - x_lo) * HALF, HALF), HALF)
        parts = [blocks[array][:, at : at + width] for array, at, width in sources]
        value = (jnp.concatenate(parts, axis=1) if len(parts) > 1 else parts[0]).astype(F32)
        square_sum = value * value
        squares[rows, :] += sum(square_sum[:, j * 128 : (j + 1) * 128] for j in range(wide // 128))
        scaled = (value * gain[:, pl.ds(starts[i], wide)]).astype(BF16)
        total[rows, :] += dot(scaled, held[i])
    if last:
        proj, gate = square, acc
        mean = jnp.sum(squares[...], axis=1, keepdims=True) * (1.0 / D)
        result = (total[...] * lax.rsqrt(mean + EPSILON)).astype(BF16)
        proj[...] = result[:, INNER:]
        gate[...] = result[:, :INNER]


def mix(place, gain, weights, steps, before=None, last=False):
    blocks, plan = [], []
    for k, own, sources in steps:
        found = []
        for array, at, width in sources:
            known = [i for i, block in enumerate(blocks) if block is array]
            if not known:
                known = [len(blocks)]
                blocks.append(array)
            found.append((known[0], at, width))
        plan.append((k, own, tuple(found)))
    apart = len({k for k, _, _ in steps})
    sums = [(ROWS, 128), (ROWS, MIXED)]
    if last:
        out = [
            jax.ShapeDtypeStruct((ROWS, MIXED - INNER), BF16),
            jax.ShapeDtypeStruct((ROWS, INNER), BF16),
        ]
    else:
        out = [jax.ShapeDtypeStruct(shape, F32) for shape in sums]
    scratch = [
        pltpu.VMEM((apart, D // Z, MIXED), BF16),
        pltpu.SemaphoreType.DMA((apart,)),
    ]
    if last:
        scratch += [pltpu.VMEM(sums[1], F32), pltpu.VMEM(sums[0], F32)]
    flops = 2 * HALF * (D // Z) * MIXED * len(steps)
    return pl.pallas_call(
        functools.partial(mix_kernel, tuple(plan), before is None, last),
        out_shape=out,
        in_specs=[whole(pltpu.SMEM), whole(), whole(pl.ANY)]
        + [whole()] * (len(blocks) + (0 if before is None else 2)),
        out_specs=[whole()] * 2,
        scratch_shapes=scratch,
        compiler_params=pltpu.CompilerParams(vmem_limit_bytes=40 * MIB),
        cost_estimate=pl.CostEstimate(
            flops=flops, bytes_accessed=1_500_000 * apart + 6_000_000, transcendentals=0
        ),
        name="mix_last" if last else "mix",
    )(place, gain, weights, *blocks, *(before or ()))


def project_stream(place, gain, weights, piece):
    wide = piece.shape[1]
    half = wide // 2
    tie = lax.optimization_barrier

    def joined(*blocks):
        return jnp.concatenate(blocks, axis=1)

    up, down, other_0 = tie((z_step(piece, 1), z_step(piece, -1), x_swap(piece)))
    left = other_0[:, :half]
    near_up, near_down = (up, 0), (down, 0)
    up, down = joined(up, left), joined(left, down)
    near = {0: ((piece, 0, wide),), 7: ((*near_up, wide),), 1: ((*near_down, wide),)}
    other = {0: ((other_0, 0, wide),)}
    sums = None
    for k in (1, 2):
        right = joined(up[:, half:wide], down[:, wide:])
        got = (z_step(up, 1), z_step(down, -1), x_swap(right))
        if k == 2:
            early = [(0, True, near[0]), (0, False, other[0])]
            early += [(j, own, from_[j]) for j in (7, 1) for own, from_ in ((True, near), (False, other))]
            early += [(j, True, near[j]) for j in (6, 2)]
            got = tie((*got, *mix(place, gain, weights, early)))
            got, sums = got[:3], got[3:]
        else:
            got = tie(got)
        up, down, right = got
        near[7 - k], near[k + 1] = ((up, 0, wide),), ((down, half, wide),)
        other[8 - k] = (up, wide, half), (right, 0, half)
        other[k] = (down, 0, half), (right, half, half)
    middle = [(k, True, near[k]) for k in (5, 3)] + [(k, False, other[k]) for k in (6, 2)]
    right = joined(up[:, half:wide], down[:, wide:])
    up, down, right, sums = tie(
        (
            z_step(up[:, half:], 1),
            z_step(down[:, :wide], -1),
            x_swap(right),
            mix(place, gain, weights, middle, sums),
        )
    )
    near[4] = (down, half, half), (up, 0, half)
    other[5] = (up, half, half), (right, 0, half)
    other[3] = (down, 0, half), (right, half, half)
    left, right = z_step(up[:, half:], 1), x_swap(up[:, :half])
    late = [(4, True, near[4])] + [(k, False, other[k]) for k in (5, 3)]
    sums = mix(place, gain, weights, late, sums)
    far = [(4, False, ((left, 0, half), (right, 0, half)))]
    return other_0, mix(place, gain, weights, far, sums, last=True)


INNER = 512
WIDE = INNER + 2 * STATE


def silu(values):
    return values / (1.0 + jnp.exp(-values))


def per_channel(values):
    head = lax.broadcasted_iota(jnp.int32, (128, INNER), 0)
    channel = lax.broadcasted_iota(jnp.int32, (128, INNER), 1)
    spread = (head == channel // SSM_HEAD_DIM).astype(BF16)
    return dot(values.astype(BF16), spread)


def conv_kernel(proj, tail, weight, bias, dt_bias, a_log, x_out, bc_out, cum_out, dt_out, msg, pad):
    pad[0:TAIL, :] = tail[...].astype(F32)
    pad[TAIL:, :] = proj[:, 0:WIDE].astype(F32)
    summed = bias[...] + weight[0:1, :] * pad[pl.ds(TAIL - CONV + 1, ROWS), :]
    for k in range(1, CONV):
        summed = summed + weight[k : k + 1, :] * pad[pl.ds(TAIL - CONV + 1 + k, ROWS), :]
    conv = silu(summed).astype(BF16)
    x_out[...] = conv[:, :INNER]
    bc_out[...] = conv[:, INNER:]
    raw = proj[:, WIDE:].astype(F32) + dt_bias[...]
    step = jnp.maximum(raw, 0.0) + jnp.log1p(jnp.exp(-jnp.abs(raw)))
    dt_out[...] = step
    rate = -jnp.exp(a_log[...]) * step
    later = lax.broadcasted_iota(jnp.int32, (BLOCK, BLOCK), 0)
    earlier = lax.broadcasted_iota(jnp.int32, (BLOCK, BLOCK), 1)
    lower = (later >= earlier).astype(F32)
    base = jnp.zeros((1, 128), F32)
    for k in range(ROWS // BLOCK):
        rows = slice(k * BLOCK, (k + 1) * BLOCK)
        here = dot(lower, rate[rows], precision=HIGHEST) + base
        cum_out[rows, :] = here
        base = here[BLOCK - 1 : BLOCK, :]
    left = step * jnp.exp(base - cum_out[...])
    weighted = (x_out[...].astype(F32) * per_channel(left)).astype(BF16)
    msg[0:STATE, :] = dot(bc_out[:, :STATE], weighted, ((0,), (0,))).astype(BF16)
    msg[STATE:, :] = per_channel(jnp.broadcast_to(jnp.exp(base), (16, 128))).astype(BF16)


def conv_and_state(proj, tail, weight, bias, dt_bias, a_log):
    return pl.pallas_call(
        conv_kernel,
        out_shape=(
            jax.ShapeDtypeStruct((ROWS, INNER), BF16),
            jax.ShapeDtypeStruct((ROWS, 2 * STATE), BF16),
            jax.ShapeDtypeStruct((ROWS, 128), F32),
            jax.ShapeDtypeStruct((ROWS, 128), F32),
            jax.ShapeDtypeStruct((MSG, INNER), BF16),
        ),
        in_specs=[whole()] * 6,
        out_specs=(whole(),) * 5,
        scratch_shapes=[pltpu.VMEM((ROWS + TAIL, WIDE), F32)],
        compiler_params=pltpu.CompilerParams(vmem_limit_bytes=32 * MIB),
        cost_estimate=pl.CostEstimate(
            flops=200_000_000, bytes_accessed=3_000_000, transcendentals=800_000
        ),
        name="conv_and_state",
    )(proj, tail, weight, bias, dt_bias, a_log)


def scan_kernel(x_ref, bc, cum, step, d_skip, out):
    lower = lax.broadcasted_iota(jnp.int32, (BLOCK, BLOCK), 0) >= lax.broadcasted_iota(
        jnp.int32, (BLOCK, BLOCK), 1
    )
    low_lane = lax.broadcasted_iota(jnp.int32, (BLOCK, 128), 1) < SSM_HEAD_DIM
    state = None
    for k in range(ROWS // BLOCK):
        rows = slice(k * BLOCK, (k + 1) * BLOCK)
        b, c = bc[rows, :STATE], bc[rows, STATE:]
        x = x_ref[rows, :]
        here = cum[rows, :]
        here_t, step_t = here.T, step[rows, :].T
        met = jnp.where(lower, dot(c, b, ((1,), (1,))), 0.0)
        parts = []
        for pair in range(4):
            left = []
            for h in (2 * pair, 2 * pair + 1):
                gap = jnp.minimum(here[:, h : h + 1] - here_t[h : h + 1, :], 0.0)
                left.append((met * jnp.exp(gap) * step_t[h : h + 1, :]).astype(BF16))
            xs = x[:, pair * 128 : (pair + 1) * 128]
            none = jnp.zeros_like(xs)
            right = jnp.concatenate([jnp.where(low_lane, xs, none), jnp.where(low_lane, none, xs)], 0)
            parts.append(dot(jnp.concatenate(left, axis=1), right))
        y = jnp.concatenate(parts, axis=1)
        last = here[BLOCK - 1 : BLOCK, :]
        if k:
            start = cum[k * BLOCK - 1 : k * BLOCK, :]
            y = y + dot(c, state.astype(BF16)) * per_channel(jnp.exp(here - start))
        out[rows, :] = y + d_skip[...] * x.astype(F32)
        if k < ROWS // BLOCK - 1:
            weighted = per_channel(step[rows, :] * jnp.exp(last - here)) * x.astype(F32)
            added = dot(b, weighted.astype(BF16), ((0,), (0,)))
            if k:
                kept = per_channel(jnp.broadcast_to(jnp.exp(last - start), (8, 128)))[0:1, :]
                state = state * kept + added
            else:
                state = added


def local_scan(x, bc, cum, step, d_skip):
    return pl.pallas_call(
        scan_kernel,
        out_shape=jax.ShapeDtypeStruct((ROWS, INNER), F32),
        in_specs=[whole()] * 5,
        out_specs=whole(),
        compiler_params=pltpu.CompilerParams(vmem_limit_bytes=32 * MIB),
        cost_estimate=pl.CostEstimate(
            flops=400_000_000, bytes_accessed=3_000_000, transcendentals=600_000
        ),
        name="local_scan",
    )(x, bc, cum, step, d_skip)


def gate_kernel(y, bc, cum, state, gate, out):
    carried = dot(bc[:, STATE:], state[...]) * per_channel(jnp.exp(cum[...]))
    out[...] = ((y[...] + carried) * silu(gate[...].astype(F32))).astype(BF16)


def finish(y, bc, cum, state, gate):
    return pl.pallas_call(
        gate_kernel,
        out_shape=jax.ShapeDtypeStruct((ROWS, INNER), BF16),
        in_specs=[whole()] * 5,
        out_specs=whole(),
        compiler_params=pltpu.CompilerParams(vmem_limit_bytes=32 * MIB),
        cost_estimate=pl.CostEstimate(
            flops=70_000_000, bytes_accessed=3_500_000, transcendentals=600_000
        ),
        name="gate",
    )(y, bc, cum, state, gate)


def then(earlier, later):
    return (earlier[0] * later[1] + later[0], earlier[1] * later[1])


def unpack(message):
    values = message.astype(F32)
    return values[:STATE], values[STATE : STATE + 1]


def packed(state, decay):
    rows = jnp.broadcast_to(decay, (16, decay.shape[1]))
    return jnp.concatenate([state, rows]).astype(BF16)


def meet(part, exchange, here):
    mine, theirs = unpack(part), unpack(exchange(part))
    first = tuple(jnp.where(here == 0, a, b) for a, b in zip(mine, theirs))
    second = tuple(jnp.where(here == 0, b, a) for a, b in zip(mine, theirs))
    before = (jnp.where(here == 0, 0.0, theirs[0]), jnp.where(here == 0, 1.0, theirs[1]))
    return before, then(first, second)


def earlier_state(message, ctx, beside):
    core, x_hi = jnp.bitwise_and(ctx, 1), jnp.bitwise_and(ctx // 2, 1)
    half = INNER // 2

    def mine(values):
        return lax.dynamic_slice_in_dim(values, core * half, half, 1)

    in_chip, chip = meet(message, lambda m: ctx_permute(m, lambda i: i ^ 1), core)
    chip = mine(packed(*chip))
    (theirs, beside) = lax.optimization_barrier((ctx_permute(chip, lambda i: i ^ 2), beside))
    in_pair, pair = meet(chip, lambda m: theirs, x_hi)
    pair = packed(*pair)
    near, mid, far = [
        unpack(lax.ppermute(pair, "ctx", [(i, i + 4 * d) for i in range(16 - 4 * d)]))
        for d in (1, 2, 3)
    ]
    incoming = then(then(then(far, mid), near), in_pair)[0].astype(BF16)
    across = ctx_permute(incoming, lambda i: i ^ 1)
    incoming = jnp.where(
        core == 0,
        jnp.concatenate([incoming, across], axis=1),
        jnp.concatenate([across, incoming], axis=1),
    )
    return (incoming.astype(F32) * in_chip[1] + in_chip[0]).astype(BF16), beside


def shards(
    query,
    key,
    value,
    out_weight,
    residual,
    norm_gain,
    w_zx,
    w_bc,
    w_dt,
    conv_x_weight,
    conv_x_bias,
    conv_bc_weight,
    conv_bc_bias,
    dt_bias,
    a_log,
    d_skip,
):
    tp, ctx = lax.axis_index("tp"), lax.axis_index("ctx")
    z, x_lo = tp // 2, jnp.bitwise_and(tp, 1)
    place = jnp.stack([ctx, x_lo * HALF, z, x_lo]).astype(jnp.int32)

    core = jnp.bitwise_and(ctx, 1)
    tie = lax.optimization_barrier
    mine = pack(place, key, value)
    mine, w_zx, w_bc, w_dt, query, w_send = tie((mine, w_zx, w_bc, w_dt, query, out_weight))
    across = ctx_permute(mine, lambda i: i ^ 2)
    below, above, facing = [y_step(mine, d) for d in (1, -1, 2)]
    mine_other = ctx_permute(mine, lambda i: i ^ 1)
    q_other = x_swap(lax.dynamic_slice_in_dim(query, (1 - x_lo) * HALF, HALF, 0))
    across, w_bc = tie((across, w_bc))
    half_0 = x_swap(lax.dynamic_slice_in_dim(w_send, core * 128, EARLY, 0))
    w_send = lax.dynamic_slice_in_dim(w_send, core * 128 + EARLY, 128 - EARLY, 0)
    bc_here = lax.dynamic_slice_in_dim(w_bc, z * STATE, STATE, 2)
    w_dt = jnp.pad(w_dt, ((0, 0), (0, 120)))
    w_zx = w_zx.reshape(w_zx.shape[0], 2 * INNER)
    w_mix = jnp.concatenate([w_zx, bc_here[:, 0], bc_here[:, 1], w_dt], axis=1)
    across, below, above, facing, q_other, mine_other, half_0, w_send, w_mix = tie(
        (across, below, above, facing, q_other, mine_other, half_0, w_send, w_mix)
    )
    w_mix = lax.all_gather(w_mix, "ctx", axis=0, tiled=True)
    late = [y_step(across, d) for d in (1, -1, 2)]
    half_1 = x_swap(w_send)
    held = [mine, across, below, above, facing, mine_other]
    held += [ctx_permute(part, lambda i: i ^ 1) for part in held[1:5]]
    q_own = lax.dynamic_slice_in_dim(query, x_lo * HALF, HALF, 0)
    state = attend(place, q_own, q_other, held)
    late, state, half_1 = tie((late, state, half_1))
    rest_0, rest_1 = [ctx_permute(half, lambda i: i ^ 1) for half in (half_0, half_1)]
    late += [ctx_permute(part, lambda i: i ^ 1) for part in late]
    state, late = tie((state, late))
    context = attend(place, q_own, q_other, late, state)
    parts = project(place, context, (out_weight, half_0, half_1, rest_0, rest_1))
    attended = sum_over_z(parts)
    residual_here = lax.dynamic_slice(residual, (x_lo * HALF, z * (D // Z)), (HALF, D // Z))
    piece = (residual_here.astype(F32) + attended).astype(BF16)
    other_piece, (proj, gate_in) = project_stream(place, norm_gain[None, :], w_mix, piece)
    stream_own = lax.dynamic_slice_in_dim(piece, x_lo * 256, 256, 1)
    stream_other = lax.dynamic_slice_in_dim(other_piece, x_lo * 256, 256, 1)
    stream = jnp.where(
        x_lo == 0,
        jnp.concatenate([stream_own, stream_other], axis=0),
        jnp.concatenate([stream_other, stream_own], axis=0),
    )
    tail = lax.ppermute(proj[ROWS - TAIL :, :WIDE], "ctx", [(i, i + 1) for i in range(15)])

    bc_weight = lax.dynamic_slice_in_dim(conv_bc_weight, z * STATE, STATE, 2)
    bc_bias = lax.dynamic_slice_in_dim(conv_bc_bias, z * STATE, STATE, 1)
    taps = jnp.concatenate([conv_x_weight, bc_weight.reshape(CONV, 2 * STATE)], axis=1)
    bias = jnp.concatenate([conv_x_bias, bc_bias.reshape(2 * STATE)])[None, :]
    lanes = ((0, 120),)
    x, bc, cum, step, message = conv_and_state(
        proj, tail, taps, bias, jnp.pad(dt_bias, lanes)[None, :], jnp.pad(a_log, lanes)[None, :]
    )
    skip = jnp.repeat(d_skip, SSM_HEAD_DIM)[None, :]
    state, y = earlier_state(message, ctx, local_scan(x, bc, cum, step, skip))
    return stream, finish(y, bc, cum, state, gate_in)


def solution(mesh):
    return jax.shard_map(
        shards,
        mesh=mesh,
        in_specs=(
            P("ctx", "tp"),
            P("ctx", None),
            P("ctx", None),
            P("tp", None),
            P("ctx", None),
            P(),
            P("ctx", None, "tp"),
            P("ctx", None, None),
            P("ctx", "tp"),
            P(None, "tp"),
            P("tp"),
            P(),
            P(),
            P("tp"),
            P("tp"),
            P("tp"),
        ),
        out_specs=(P("ctx", "tp"), P("ctx", "tp")),
        check_vma=False,
    )
```

```python
import functools
import math

import jax
import jax.numpy as jnp
from jax import lax
from jax.experimental import pallas as pl
from jax.experimental.pallas import tpu as pltpu
from jax.sharding import PartitionSpec as P

D = 4096
HEAD_DIM = 128
SSM_HEAD_DIM = 64
STATE = 128
CONV = 4
BLOCK = 128
NEG_BIG = -1e30
EPSILON = 1e-05
HIGHEST = lax.Precision.HIGHEST
F32 = jnp.float32
BF16 = jnp.bfloat16
MIB = 1024 * 1024

Y, Z = 4, 8
ROWS = 512
HALF = 256
EARLY = 48
TAIL = 16
MSG = STATE + 16


def ctx_permute(block, move):
    return lax.ppermute(block, "ctx", [(i, move(i)) for i in range(16)])


def tp_permute(block, move):
    return lax.ppermute(block, "tp", [(i, move(i)) for i in range(16)])


def y_step(block, d):
    return ctx_permute(block, lambda i: (i + 4 * d) % 16)


def z_step(block, d):
    return tp_permute(block, lambda i: (i + 2 * d) % 16)


def x_swap(block):
    return tp_permute(block, lambda i: i ^ 1)


def dot(a, b, dims=((1,), (0,)), precision=None):
    return lax.dot_general(a, b, (dims, ((), ())), precision=precision, preferred_element_type=F32)


def whole(memory=pltpu.VMEM):
    return pl.BlockSpec(memory_space=memory)


def pack_kernel(place, key, value, out):
    del place
    out[0:ROWS, :] = key[...]
    for j in range(4):
        rows = slice(j * HEAD_DIM, (j + 1) * HEAD_DIM)
        out[ROWS + j * HEAD_DIM : ROWS + (j + 1) * HEAD_DIM, :] = value[rows, :].T


def pack(place, key, value):
    column = pl.BlockSpec((ROWS, HEAD_DIM), lambda i, place: (0, place[2]))
    return pl.pallas_call(
        pack_kernel,
        out_shape=jax.ShapeDtypeStruct((2 * ROWS, HEAD_DIM), BF16),
        grid_spec=pltpu.PrefetchScalarGridSpec(
            num_scalar_prefetch=1,
            grid=(1,),
            in_specs=[column, column],
            out_specs=pl.BlockSpec((2 * ROWS, HEAD_DIM), lambda i, place: (0, 0)),
        ),
        name="pack",
    )(place, key, value)


FIRST = ((0, 0), (0, 1), (3, 0), (1, 0), (2, 0))
SECOND = ((3, 1), (1, 1), (2, 1))


def attend_kernel(homes, last, place, q_own, q_other, *refs):
    count = 2 * len(homes)
    pieces, refs = refs[:count], refs[count:]
    if last:
        (top_in, total_in, acc_in, out), (kv, top, total, acc) = refs[:4], refs[4:]
        top[...] = top_in[...]
        total[...] = total_in[...]
        acc[...] = acc_in[...]
    else:
        top, total, acc, kv = refs
        top[...] = jnp.full(top.shape, NEG_BIG, F32)
        total[...] = jnp.zeros(total.shape, F32)
        acc[...] = jnp.zeros(acc.shape, F32)
    me, x_lo = place[0], place[3]
    for slot, piece in enumerate(pieces):
        kv[slot] = piece[...]
    unit = math.log2(math.e) / math.sqrt(HEAD_DIM)

    def block(slot, masked):
        keys = kv[slot, 0:ROWS, :]
        values = jnp.concatenate(
            [kv[slot, ROWS + HEAD_DIM * j : ROWS + HEAD_DIM * (j + 1), :] for j in range(4)], axis=1
        )
        heads = range(4)
        scores = []
        for h in heads:
            source = q_own if h < 2 else q_other
            queries = source[:, (h % 2) * HEAD_DIM : (h % 2 + 1) * HEAD_DIM]
            scores.append(dot(keys, queries, ((1,), (1,))))
        if masked:
            key_at = lax.broadcasted_iota(jnp.int32, scores[0].shape, 0)
            row_at = lax.broadcasted_iota(jnp.int32, scores[0].shape, 1) + x_lo * HALF
            visible = key_at <= row_at
            scores = [jnp.where(visible, score, NEG_BIG) for score in scores]
        old = [top[h] for h in heads]
        new = [jnp.maximum(old[h], jnp.max(scores[h], axis=0, keepdims=True)) for h in heads]
        weights = [jnp.exp2((scores[h] - new[h]) * unit) for h in heads]
        factor = [jnp.exp2((old[h] - new[h]) * unit) for h in heads]
        sums = [jnp.sum(weights[h], axis=0, keepdims=True) for h in heads]
        mixed = [dot(values, weights[h].astype(BF16)) for h in heads]
        for h in heads:
            total[h] = total[h] * factor[h] + sums[h]
            acc[h] = acc[h] * factor[h] + mixed[h]
            top[h] = new[h]

    if not last:
        block(0, True)
    each = len(homes)
    aparts = sum(apart << (2 * i) for i, (apart, _) in enumerate(homes))
    crosses = sum(crossed << (2 * i) for i, (_, crossed) in enumerate(homes))

    @pl.loop(0 if last else 1, 2 * each)
    def _(slot):
        other = (slot >= each).astype(jnp.int32)
        shift = 2 * (slot - other * each)
        apart = jnp.bitwise_and(lax.shift_right_logical(jnp.int32(aparts), shift), 3)
        crossed = jnp.bitwise_and(lax.shift_right_logical(jnp.int32(crosses), shift), 3)
        y = jnp.bitwise_and(me // 4 + apart, 3)
        rest = jnp.bitwise_xor(jnp.bitwise_and(me, 3), crossed * 2 + other)

        @pl.when(y * 4 + rest < me)
        def _():
            block(slot, False)

    if last:
        for h in range(4):
            out[:, h * HEAD_DIM : (h + 1) * HEAD_DIM] = (acc[h] / total[h]).T.astype(BF16)


def attend(place, q_own, q_other, pieces, before=None):
    last = before is not None
    state = [
        jax.ShapeDtypeStruct((4, 1, HALF), F32),
        jax.ShapeDtypeStruct((4, 1, HALF), F32),
        jax.ShapeDtypeStruct((4, HEAD_DIM, HALF), F32),
    ]
    scratch = [pltpu.VMEM((len(pieces), 2 * ROWS, HEAD_DIM), BF16)]
    if last:
        scratch += [pltpu.VMEM(part.shape, part.dtype) for part in state]
    return pl.pallas_call(
        functools.partial(attend_kernel, SECOND if last else FIRST, last),
        out_shape=jax.ShapeDtypeStruct((HALF, 4 * HEAD_DIM), BF16) if last else state,
        in_specs=[whole(pltpu.SMEM), whole(), whole()]
        + [whole()] * (len(pieces) + (3 if last else 0)),
        out_specs=whole() if last else [whole()] * 3,
        scratch_shapes=scratch,
        compiler_params=pltpu.CompilerParams(vmem_limit_bytes=32 * MIB),
        cost_estimate=pl.CostEstimate(
            flops=1_000_000, bytes_accessed=1_000_000, transcendentals=0
        ),
        name="attend_rest" if last else "attend_first",
    )(place, q_own, q_other, *pieces, *(before or ()))


def project_kernel(place, context, w_own, half_0, half_1, rest_0, rest_1, *refs):
    parts, weight = refs[:9], refs[9]
    core, z = jnp.bitwise_and(place[0], 1), place[2]
    weight[0:HALF, :] = w_own[...]
    for first, second, which in ((half_0, half_1, core), (rest_0, rest_1, 1 - core)):
        start = pl.multiple_of(HALF + which * 128, 128)
        weight[pl.ds(start, EARLY), :] = first[...]
        weight[pl.ds(start + EARLY, 128 - EARLY), :] = second[...]
    wide = D // Z
    for k in range(Z):
        column = pl.multiple_of(jnp.bitwise_and(z + k, Z - 1) * wide, wide)
        part = dot(context[...], weight[:, pl.ds(column, wide)]).astype(BF16)
        if k == 4:
            parts[4][...] = part[:, : wide // 2]
            parts[8][...] = part[:, wide // 2 :]
        else:
            parts[k][...] = part


def project(place, context, weights):
    wide = D // Z
    out = [jax.ShapeDtypeStruct((HALF, wide // 2 if k in (4, 8) else wide), BF16) for k in range(9)]
    return pl.pallas_call(
        project_kernel,
        out_shape=out,
        in_specs=[whole(pltpu.SMEM)] + [whole()] * 6,
        out_specs=[whole()] * 9,
        scratch_shapes=[pltpu.VMEM((ROWS, D), BF16)],
        compiler_params=pltpu.CompilerParams(vmem_limit_bytes=32 * MIB),
        cost_estimate=pl.CostEstimate(
            flops=1_100_000_000, bytes_accessed=6_500_000, transcendentals=0
        ),
        name="project",
    )(place, context, *weights)


def sum_over_z(parts):
    half = parts[4].shape[1]
    up, down = z_step(parts[4], 1), z_step(parts[8], -1)
    third, fifth = parts[3].astype(F32), parts[5].astype(F32)
    up = jnp.concatenate([third[:, :half] + up.astype(F32), third[:, half:]], axis=1)
    down = jnp.concatenate([fifth[:, :half], fifth[:, half:] + down.astype(F32)], axis=1)
    for k in (2, 1, 0):
        up, down = lax.optimization_barrier((up.astype(BF16), down.astype(BF16)))
        up, down = z_step(up, 1), z_step(down, -1)
        if k:
            up = parts[k].astype(F32) + up.astype(F32)
            down = parts[8 - k].astype(F32) + down.astype(F32)
    return parts[0].astype(F32) + up.astype(F32) + down.astype(F32)


MIXED = 1408


def mix_kernel(steps, first, last, place, gain, weights, *refs):
    count = 1 + max(array for _, _, sources in steps for array, _, _ in sources)
    blocks, refs = refs[:count], refs[count:]
    if not first:
        (square_in, acc_in), refs = refs[:2], refs[2:]
    (square, acc), (held, sems) = refs[:2], refs[2:4]
    if last:
        total, squares = refs[4], refs[5]
    else:
        total, squares = acc, square
    z, x_lo = place[2], place[3]
    wide = D // Z
    apart = []
    for k, _, _ in steps:
        if k not in apart:
            apart.append(k)
    starts = [pl.multiple_of(jnp.bitwise_and(z + k, Z - 1) * wide, wide) for k in apart]
    copies = [
        pltpu.make_async_copy(weights.at[pl.ds(start, wide)], held.at[i], sems.at[i])
        for i, start in enumerate(starts)
    ]
    for copy in copies:
        copy.start()
    if first:
        squares[...] = jnp.zeros(squares.shape, F32)
        total[...] = jnp.zeros(total.shape, F32)
    else:
        squares[...] = square_in[...]
        total[...] = acc_in[...]
    waited = set()
    for k, own, sources in steps:
        i = apart.index(k)
        if k not in waited:
            waited.add(k)
            copies[i].wait()
        rows = pl.ds(pl.multiple_of((x_lo if own else 1 - x_lo) * HALF, HALF), HALF)
        parts = [blocks[array][:, at : at + width] for array, at, width in sources]
        value = (jnp.concatenate(parts, axis=1) if len(parts) > 1 else parts[0]).astype(F32)
        square_sum = value * value
        squares[rows, :] += sum(square_sum[:, j * 128 : (j + 1) * 128] for j in range(wide // 128))
        scaled = (value * gain[:, pl.ds(starts[i], wide)]).astype(BF16)
        total[rows, :] += dot(scaled, held[i])
    if last:
        proj, gate = square, acc
        mean = jnp.sum(squares[...], axis=1, keepdims=True) * (1.0 / D)
        result = (total[...] * lax.rsqrt(mean + EPSILON)).astype(BF16)
        proj[...] = result[:, INNER:]
        gate[...] = result[:, :INNER]


def mix(place, gain, weights, steps, before=None, last=False):
    blocks, plan = [], []
    for k, own, sources in steps:
        found = []
        for array, at, width in sources:
            known = [i for i, block in enumerate(blocks) if block is array]
            if not known:
                known = [len(blocks)]
                blocks.append(array)
            found.append((known[0], at, width))
        plan.append((k, own, tuple(found)))
    apart = len({k for k, _, _ in steps})
    sums = [(ROWS, 128), (ROWS, MIXED)]
    if last:
        out = [
            jax.ShapeDtypeStruct((ROWS, MIXED - INNER), BF16),
            jax.ShapeDtypeStruct((ROWS, INNER), BF16),
        ]
    else:
        out = [jax.ShapeDtypeStruct(shape, F32) for shape in sums]
    scratch = [
        pltpu.VMEM((apart, D // Z, MIXED), BF16),
        pltpu.SemaphoreType.DMA((apart,)),
    ]
    if last:
        scratch += [pltpu.VMEM(sums[1], F32), pltpu.VMEM(sums[0], F32)]
    flops = 2 * HALF * (D // Z) * MIXED * len(steps)
    return pl.pallas_call(
        functools.partial(mix_kernel, tuple(plan), before is None, last),
        out_shape=out,
        in_specs=[whole(pltpu.SMEM), whole(), whole(pl.ANY)]
        + [whole()] * (len(blocks) + (0 if before is None else 2)),
        out_specs=[whole()] * 2,
        scratch_shapes=scratch,
        compiler_params=pltpu.CompilerParams(vmem_limit_bytes=40 * MIB),
        cost_estimate=pl.CostEstimate(
            flops=flops, bytes_accessed=1_500_000 * apart + 6_000_000, transcendentals=0
        ),
        name="mix_last" if last else "mix",
    )(place, gain, weights, *blocks, *(before or ()))


def project_stream(place, gain, weights, piece):
    wide = piece.shape[1]
    half = wide // 2
    tie = lax.optimization_barrier

    def joined(*blocks):
        return jnp.concatenate(blocks, axis=1)

    up, down, other_0 = tie((z_step(piece, 1), z_step(piece, -1), x_swap(piece)))
    left = other_0[:, :half]
    near_up, near_down = (up, 0), (down, 0)
    up, down = joined(up, left), joined(left, down)
    near = {0: ((piece, 0, wide),), 7: ((*near_up, wide),), 1: ((*near_down, wide),)}
    other = {0: ((other_0, 0, wide),)}
    sums = None
    for k in (1, 2):
        right = joined(up[:, half:wide], down[:, wide:])
        got = (z_step(up, 1), z_step(down, -1), x_swap(right))
        if k == 2:
            early = [(0, True, near[0]), (0, False, other[0])]
            early += [(j, own, from_[j]) for j in (7, 1) for own, from_ in ((True, near), (False, other))]
            early += [(j, True, near[j]) for j in (6, 2)]
            got = tie((*got, *mix(place, gain, weights, early)))
            got, sums = got[:3], got[3:]
        else:
            got = tie(got)
        up, down, right = got
        near[7 - k], near[k + 1] = ((up, 0, wide),), ((down, half, wide),)
        other[8 - k] = (up, wide, half), (right, 0, half)
        other[k] = (down, 0, half), (right, half, half)
    middle = [(k, True, near[k]) for k in (5, 3)] + [(k, False, other[k]) for k in (6, 2)]
    right = joined(up[:, half:wide], down[:, wide:])
    up, down, right, sums = tie(
        (
            z_step(up[:, half:], 1),
            z_step(down[:, :wide], -1),
            x_swap(right),
            mix(place, gain, weights, middle, sums),
        )
    )
    near[4] = (down, half, half), (up, 0, half)
    other[5] = (up, half, half), (right, 0, half)
    other[3] = (down, 0, half), (right, half, half)
    left, right = z_step(up[:, half:], 1), x_swap(up[:, :half])
    late = [(4, True, near[4])] + [(k, False, other[k]) for k in (5, 3)]
    sums = mix(place, gain, weights, late, sums)
    far = [(4, False, ((left, 0, half), (right, 0, half)))]
    return other_0, mix(place, gain, weights, far, sums, last=True)


INNER = 512
WIDE = INNER + 2 * STATE


def silu(values):
    return values / (1.0 + jnp.exp(-values))


def per_channel(values):
    head = lax.broadcasted_iota(jnp.int32, (128, INNER), 0)
    channel = lax.broadcasted_iota(jnp.int32, (128, INNER), 1)
    spread = (head == channel // SSM_HEAD_DIM).astype(BF16)
    return dot(values.astype(BF16), spread)


def conv_kernel(proj, tail, weight, bias, dt_bias, a_log, x_out, bc_out, cum_out, dt_out, msg, pad):
    pad[0:TAIL, :] = tail[...].astype(F32)
    pad[TAIL:, :] = proj[:, 0:WIDE].astype(F32)
    summed = bias[...] + weight[0:1, :] * pad[pl.ds(TAIL - CONV + 1, ROWS), :]
    for k in range(1, CONV):
        summed = summed + weight[k : k + 1, :] * pad[pl.ds(TAIL - CONV + 1 + k, ROWS), :]
    conv = silu(summed).astype(BF16)
    x_out[...] = conv[:, :INNER]
    bc_out[...] = conv[:, INNER:]
    raw = proj[:, WIDE:].astype(F32) + dt_bias[...]
    step = jnp.maximum(raw, 0.0) + jnp.log1p(jnp.exp(-jnp.abs(raw)))
    dt_out[...] = step
    rate = -jnp.exp(a_log[...]) * step
    later = lax.broadcasted_iota(jnp.int32, (BLOCK, BLOCK), 0)
    earlier = lax.broadcasted_iota(jnp.int32, (BLOCK, BLOCK), 1)
    lower = (later >= earlier).astype(F32)
    base = jnp.zeros((1, 128), F32)
    for k in range(ROWS // BLOCK):
        rows = slice(k * BLOCK, (k + 1) * BLOCK)
        here = dot(lower, rate[rows], precision=HIGHEST) + base
        cum_out[rows, :] = here
        base = here[BLOCK - 1 : BLOCK, :]
    left = step * jnp.exp(base - cum_out[...])
    weighted = (x_out[...].astype(F32) * per_channel(left)).astype(BF16)
    msg[0:STATE, :] = dot(bc_out[:, :STATE], weighted, ((0,), (0,))).astype(BF16)
    msg[STATE:, :] = per_channel(jnp.broadcast_to(jnp.exp(base), (16, 128))).astype(BF16)


def conv_and_state(proj, tail, weight, bias, dt_bias, a_log):
    return pl.pallas_call(
        conv_kernel,
        out_shape=(
            jax.ShapeDtypeStruct((ROWS, INNER), BF16),
            jax.ShapeDtypeStruct((ROWS, 2 * STATE), BF16),
            jax.ShapeDtypeStruct((ROWS, 128), F32),
            jax.ShapeDtypeStruct((ROWS, 128), F32),
            jax.ShapeDtypeStruct((MSG, INNER), BF16),
        ),
        in_specs=[whole()] * 6,
        out_specs=(whole(),) * 5,
        scratch_shapes=[pltpu.VMEM((ROWS + TAIL, WIDE), F32)],
        compiler_params=pltpu.CompilerParams(vmem_limit_bytes=32 * MIB),
        cost_estimate=pl.CostEstimate(
            flops=200_000_000, bytes_accessed=3_000_000, transcendentals=800_000
        ),
        name="conv_and_state",
    )(proj, tail, weight, bias, dt_bias, a_log)


def scan_kernel(x_ref, bc, cum, step, d_skip, out):
    lower = lax.broadcasted_iota(jnp.int32, (BLOCK, BLOCK), 0) >= lax.broadcasted_iota(
        jnp.int32, (BLOCK, BLOCK), 1
    )
    low_lane = lax.broadcasted_iota(jnp.int32, (BLOCK, 128), 1) < SSM_HEAD_DIM
    state = None
    for k in range(ROWS // BLOCK):
        rows = slice(k * BLOCK, (k + 1) * BLOCK)
        b, c = bc[rows, :STATE], bc[rows, STATE:]
        x = x_ref[rows, :]
        here = cum[rows, :]
        here_t, step_t = here.T, step[rows, :].T
        met = jnp.where(lower, dot(c, b, ((1,), (1,))), 0.0)
        parts = []
        for pair in range(4):
            left = []
            for h in (2 * pair, 2 * pair + 1):
                gap = jnp.minimum(here[:, h : h + 1] - here_t[h : h + 1, :], 0.0)
                left.append((met * jnp.exp(gap) * step_t[h : h + 1, :]).astype(BF16))
            xs = x[:, pair * 128 : (pair + 1) * 128]
            none = jnp.zeros_like(xs)
            right = jnp.concatenate([jnp.where(low_lane, xs, none), jnp.where(low_lane, none, xs)], 0)
            parts.append(dot(jnp.concatenate(left, axis=1), right))
        y = jnp.concatenate(parts, axis=1)
        last = here[BLOCK - 1 : BLOCK, :]
        if k:
            start = cum[k * BLOCK - 1 : k * BLOCK, :]
            y = y + dot(c, state.astype(BF16)) * per_channel(jnp.exp(here - start))
        out[rows, :] = y + d_skip[...] * x.astype(F32)
        if k < ROWS // BLOCK - 1:
            weighted = per_channel(step[rows, :] * jnp.exp(last - here)) * x.astype(F32)
            added = dot(b, weighted.astype(BF16), ((0,), (0,)))
            if k:
                kept = per_channel(jnp.broadcast_to(jnp.exp(last - start), (8, 128)))[0:1, :]
                state = state * kept + added
            else:
                state = added


def local_scan(x, bc, cum, step, d_skip):
    return pl.pallas_call(
        scan_kernel,
        out_shape=jax.ShapeDtypeStruct((ROWS, INNER), F32),
        in_specs=[whole()] * 5,
        out_specs=whole(),
        compiler_params=pltpu.CompilerParams(vmem_limit_bytes=32 * MIB),
        cost_estimate=pl.CostEstimate(
            flops=400_000_000, bytes_accessed=3_000_000, transcendentals=600_000
        ),
        name="local_scan",
    )(x, bc, cum, step, d_skip)


def gate_kernel(y, bc, cum, state, gate, out):
    carried = dot(bc[:, STATE:], state[...]) * per_channel(jnp.exp(cum[...]))
    out[...] = ((y[...] + carried) * silu(gate[...].astype(F32))).astype(BF16)


def finish(y, bc, cum, state, gate):
    return pl.pallas_call(
        gate_kernel,
        out_shape=jax.ShapeDtypeStruct((ROWS, INNER), BF16),
        in_specs=[whole()] * 5,
        out_specs=whole(),
        compiler_params=pltpu.CompilerParams(vmem_limit_bytes=32 * MIB),
        cost_estimate=pl.CostEstimate(
            flops=70_000_000, bytes_accessed=3_500_000, transcendentals=600_000
        ),
        name="gate",
    )(y, bc, cum, state, gate)


def then(earlier, later):
    return (earlier[0] * later[1] + later[0], earlier[1] * later[1])


def unpack(message):
    values = message.astype(F32)
    return values[:STATE], values[STATE : STATE + 1]


def packed(state, decay):
    rows = jnp.broadcast_to(decay, (16, decay.shape[1]))
    return jnp.concatenate([state, rows]).astype(BF16)


def meet(part, exchange, here):
    mine, theirs = unpack(part), unpack(exchange(part))
    first = tuple(jnp.where(here == 0, a, b) for a, b in zip(mine, theirs))
    second = tuple(jnp.where(here == 0, b, a) for a, b in zip(mine, theirs))
    before = (jnp.where(here == 0, 0.0, theirs[0]), jnp.where(here == 0, 1.0, theirs[1]))
    return before, then(first, second)


def earlier_state(message, ctx, beside):
    core, x_hi = jnp.bitwise_and(ctx, 1), jnp.bitwise_and(ctx // 2, 1)
    half = INNER // 2

    def mine(values):
        return lax.dynamic_slice_in_dim(values, core * half, half, 1)

    in_chip, chip = meet(message, lambda m: ctx_permute(m, lambda i: i ^ 1), core)
    chip = mine(packed(*chip))
    (theirs, beside) = lax.optimization_barrier((ctx_permute(chip, lambda i: i ^ 2), beside))
    in_pair, pair = meet(chip, lambda m: theirs, x_hi)
    pair = packed(*pair)
    near, mid, far = [
        unpack(lax.ppermute(pair, "ctx", [(i, i + 4 * d) for i in range(16 - 4 * d)]))
        for d in (1, 2, 3)
    ]
    incoming = then(then(then(far, mid), near), in_pair)[0].astype(BF16)
    across = ctx_permute(incoming, lambda i: i ^ 1)
    incoming = jnp.where(
        core == 0,
        jnp.concatenate([incoming, across], axis=1),
        jnp.concatenate([across, incoming], axis=1),
    )
    return (incoming.astype(F32) * in_chip[1] + in_chip[0]).astype(BF16), beside


def shards(
    query,
    key,
    value,
    out_weight,
    residual,
    norm_gain,
    w_zx,
    w_bc,
    w_dt,
    conv_x_weight,
    conv_x_bias,
    conv_bc_weight,
    conv_bc_bias,
    dt_bias,
    a_log,
    d_skip,
):
    tp, ctx = lax.axis_index("tp"), lax.axis_index("ctx")
    z, x_lo = tp // 2, jnp.bitwise_and(tp, 1)
    place = jnp.stack([ctx, x_lo * HALF, z, x_lo]).astype(jnp.int32)

    core = jnp.bitwise_and(ctx, 1)
    tie = lax.optimization_barrier
    mine = pack(place, key, value)
    mine, w_zx, w_bc, w_dt, query, w_send = tie((mine, w_zx, w_bc, w_dt, query, out_weight))
    across = ctx_permute(mine, lambda i: i ^ 2)
    below, above, facing = [y_step(mine, d) for d in (1, -1, 2)]
    mine_other = ctx_permute(mine, lambda i: i ^ 1)
    q_other = x_swap(lax.dynamic_slice_in_dim(query, (1 - x_lo) * HALF, HALF, 0))
    across, w_bc = tie((across, w_bc))
    half_0 = x_swap(lax.dynamic_slice_in_dim(w_send, core * 128, EARLY, 0))
    w_send = lax.dynamic_slice_in_dim(w_send, core * 128 + EARLY, 128 - EARLY, 0)
    bc_here = lax.dynamic_slice_in_dim(w_bc, z * STATE, STATE, 2)
    w_dt = jnp.pad(w_dt, ((0, 0), (0, 120)))
    w_zx = w_zx.reshape(w_zx.shape[0], 2 * INNER)
    w_mix = jnp.concatenate([w_zx, bc_here[:, 0], bc_here[:, 1], w_dt], axis=1)
    q_other, w_mix = tie((q_other, w_mix))
    across, below, above, facing, q_other, mine_other, half_0, w_send = tie(
        (across, below, above, facing, q_other, mine_other, half_0, w_send)
    )
    w_mix = lax.all_gather(w_mix, "ctx", axis=0, tiled=True)
    late = [y_step(across, d) for d in (1, -1, 2)]
    half_1 = x_swap(w_send)
    held = [mine, across, below, above, facing, mine_other]
    held += [ctx_permute(part, lambda i: i ^ 1) for part in held[1:5]]
    q_own = lax.dynamic_slice_in_dim(query, x_lo * HALF, HALF, 0)
    state = attend(place, q_own, q_other, held)
    late, state, half_1 = tie((late, state, half_1))
    rest_0, rest_1 = [ctx_permute(half, lambda i: i ^ 1) for half in (half_0, half_1)]
    late += [ctx_permute(part, lambda i: i ^ 1) for part in late]
    state, late = tie((state, late))
    context = attend(place, q_own, q_other, late, state)
    parts = project(place, context, (out_weight, half_0, half_1, rest_0, rest_1))
    attended = sum_over_z(parts)
    residual_here = lax.dynamic_slice(residual, (x_lo * HALF, z * (D // Z)), (HALF, D // Z))
    piece = (residual_here.astype(F32) + attended).astype(BF16)
    other_piece, (proj, gate_in) = project_stream(place, norm_gain[None, :], w_mix, piece)
    stream_own = lax.dynamic_slice_in_dim(piece, x_lo * 256, 256, 1)
    stream_other = lax.dynamic_slice_in_dim(other_piece, x_lo * 256, 256, 1)
    stream = jnp.where(
        x_lo == 0,
        jnp.concatenate([stream_own, stream_other], axis=0),
        jnp.concatenate([stream_other, stream_own], axis=0),
    )
    tail = lax.ppermute(proj[ROWS - TAIL :, :WIDE], "ctx", [(i, i + 1) for i in range(15)])

    bc_weight = lax.dynamic_slice_in_dim(conv_bc_weight, z * STATE, STATE, 2)
    bc_bias = lax.dynamic_slice_in_dim(conv_bc_bias, z * STATE, STATE, 1)
    taps = jnp.concatenate([conv_x_weight, bc_weight.reshape(CONV, 2 * STATE)], axis=1)
    bias = jnp.concatenate([conv_x_bias, bc_bias.reshape(2 * STATE)])[None, :]
    lanes = ((0, 120),)
    x, bc, cum, step, message = conv_and_state(
        proj, tail, taps, bias, jnp.pad(dt_bias, lanes)[None, :], jnp.pad(a_log, lanes)[None, :]
    )
    skip = jnp.repeat(d_skip, SSM_HEAD_DIM)[None, :]
    state, y = earlier_state(message, ctx, local_scan(x, bc, cum, step, skip))
    return stream, finish(y, bc, cum, state, gate_in)


def solution(mesh):
    return jax.shard_map(
        shards,
        mesh=mesh,
        in_specs=(
            P("ctx", "tp"),
            P("ctx", None),
            P("ctx", None),
            P("tp", None),
            P("ctx", None),
            P(),
            P("ctx", None, "tp"),
            P("ctx", None, None),
            P("ctx", "tp"),
            P(None, "tp"),
            P("tp"),
            P(),
            P(),
            P("tp"),
            P("tp"),
            P("tp"),
        ),
        out_specs=(P("ctx", "tp"), P("ctx", "tp")),
        check_vma=False,
    )
```
